512 devices in a mesh: vid: 64 (over y_hi, x, z), aud: 4 (over y_lo), tp: 2 (over core).
Axes of the slice: x: 4, y: 8 (y_hi: 2, y_lo: 4; y = y_hi * 4 + y_lo), z: 8, core: 2. Of those that a mesh axis runs over, the one named last changes fastest.
Arguments:
- video_proj: bfloat16 [4, 8192, 3072], P(None, ('vid', 'aud'), 'tp'), may hold values from -125 to 125
- audio_proj: bfloat16 [4, 2048, 3072], P(None, ('vid', 'aud'), 'tp'), may hold values from -125 to 125
- video_gains: float32 [3, 3072], P(None, 'tp'), may hold values from 1.2 to 2
- audio_gains: float32 [3, 3072], P(None, 'tp'), may hold values from 1.2 to 2
- cross_gates: bfloat16 [2, 50, 3072], P(None, None, 'tp'), may hold values from 0.19921875 to 2
- timestep: int32 [1], replicated, may hold values from 0 to 49
- video_counts: int32 [64], replicated, may hold values from 64 to 128, as said below
- audio_counts: int32 [64], replicated, may hold values from 16 to 32, as said below
Outputs:
- video_mixed: bfloat16 [8192, 3072], P(('vid', 'aud'), 'tp')
- audio_mixed: bfloat16 [2048, 3072], P(('vid', 'aud'), 'tp')
The draws below stay inside these ranges and needn't reach their ends.
Inputs may be any that keep to these rules, and one draw needn't show every extreme that they name: `video_counts`: entry s counts the live video tokens of vid shard s, which are its first ones; the others are padding that no query attends to; some shard is full. `audio_counts`: entry s counts the live audio tokens of vid shard s, which are its first ones; the others are padding that no query attends to; some shard is full.
All inputs are finite; a program needn't handle non-finite values.
Results may differ from the reference program's by a relative error of at most 0.011.
Values may be sent and summed in bfloat16 or wider, within the bound.
No kernel may reach another device: no remote copies, remote signals or barrier semaphores. Data moves between devices by JAX's collectives and lax.ppermute only.
A program may use at most 64 MiB of HBM per device.

```python
import math
import jax
import jax.numpy as jnp
from jax import lax

D = 3072
HEADS = 24
HD = 128
VTOK_DEV = 128
ATOK_DEV = 32
STEPS = 50
SHARDS = 64
VTOKENS = 8192
ATOKENS = 2048


def column_profile(key):
    key_order, key_spread = jax.random.split(key)
    levels = jnp.exp(jnp.arange(HEADS, dtype=jnp.float32) / max(HEADS - 1, 1) * math.log(1.25))
    order = jax.random.permutation(key_order, HEADS)
    head_levels = jnp.repeat(levels[order], HD)
    spread = jnp.exp(jax.random.uniform(key_spread, (D,), jnp.float32, 0.0, math.log(2.0)))
    return head_levels * spread


def row_profile(key, row_count):
    return jnp.exp(jax.random.uniform(key, (4, row_count, 1), jnp.float32, 0.0, math.log(3.0)))


def draw_video_proj(key, part):
    key = jax.random.fold_in(key, 11)
    key_noise, key_column, key_row = jax.random.split(key, 3)
    noise = jnp.clip(jax.random.normal(key_noise, (4, VTOKENS, D), jnp.float32), -4.0, 4.0)
    field = noise * column_profile(key_column)[None, None, :] * row_profile(key_row, VTOKENS)
    return field.astype(jnp.bfloat16)


def draw_audio_proj(key, part):
    key = jax.random.fold_in(key, 12)
    key_noise, key_column, key_row = jax.random.split(key, 3)
    noise = jnp.clip(jax.random.normal(key_noise, (4, ATOKENS, D), jnp.float32), -4.0, 4.0)
    field = noise * column_profile(key_column)[None, None, :] * row_profile(key_row, ATOKENS)
    return field.astype(jnp.bfloat16)


def draw_video_counts(key, part):
    key = jax.random.fold_in(key, 21)
    key_counts, key_full = jax.random.split(key)
    counts = jax.random.randint(key_counts, (SHARDS,), VTOK_DEV // 2, VTOK_DEV + 1)
    full_shard = jax.random.randint(key_full, (), 0, SHARDS)
    return counts.at[full_shard].set(VTOK_DEV).astype(jnp.int32)


def draw_audio_counts(key, part):
    key = jax.random.fold_in(key, 22)
    key_counts, key_full = jax.random.split(key)
    counts = jax.random.randint(key_counts, (SHARDS,), ATOK_DEV // 2, ATOK_DEV + 1)
    full_shard = jax.random.randint(key_full, (), 0, SHARDS)
    return counts.at[full_shard].set(ATOK_DEV).astype(jnp.int32)


def block_levels(stream_key, dims, cuts, smallest, top_value):
    gain = 1.0
    for dim, blocks in cuts:
        steps = jax.random.uniform(jax.random.fold_in(jax.random.fold_in(stream_key, 6), dim), (blocks,), jnp.float32, smallest / len(cuts), top_value / len(cuts))
        gain = gain * jnp.repeat(jnp.exp(steps), dims[dim] // blocks).reshape((-1,) + (1,) * (len(dims) - 1 - dim))
    return gain


def setup_inputs(seed: int = 0) -> dict:
    splits = jax.random.split(jax.random.key(seed), 9)
    return {
        "video_proj": draw_video_proj(jax.random.fold_in(splits[8], 71), 0),
        "audio_proj": draw_audio_proj(jax.random.fold_in(splits[8], 71), 0),
        "video_gains": jnp.clip(1.2 + 0.79999995 * jax.random.uniform(splits[2], (3, D), jnp.float32) ** block_levels(splits[2], (3, D), ((1, 2),), -0.2, 0.2), 1.2, 2.0),
        "audio_gains": jnp.clip(1.2 + 0.79999995 * jax.random.uniform(splits[3], (3, D), jnp.float32) ** block_levels(splits[3], (3, D), ((1, 2),), -0.2, 0.2), 1.2, 2.0),
        "cross_gates": jnp.clip(0.19921875 + 1.8007812 * jax.random.uniform(splits[4], (2, STEPS, D), jnp.float32) ** block_levels(splits[4], (2, STEPS, D), ((2, 2),), -0.2, 0.2), 0.19921875, 2.0).astype(jnp.bfloat16),
        "timestep": jax.random.randint(splits[5], (1,), 0, STEPS).astype(jnp.int32),
        "video_counts": draw_video_counts(jax.random.fold_in(splits[8], 71), 0),
        "audio_counts": draw_audio_counts(jax.random.fold_in(splits[8], 71), 0),
    }


EPSILON = 1e-06

def rms_normed(raw_rows, gain_row):
    values_f = raw_rows.astype(jnp.float32)
    mean_square = lax.optimization_barrier(jnp.mean(values_f * values_f, axis=-1, keepdims=True))
    return (values_f * lax.rsqrt(mean_square + EPSILON) * gain_row.astype(jnp.float32)).astype(jnp.bfloat16)

def live_mask(counts, tok_shard, total_rows):
    positions = jnp.arange(total_rows, dtype=jnp.int32)
    shard_of = (positions // tok_shard).astype(jnp.int32)
    within = positions - shard_of * tok_shard
    return within < counts[shard_of]

def attend(query_rows, key_rows, value_rows, allowed):
    total_q = query_rows.shape[0]
    block_len = min(1024, total_q)

    def by_head(tensor):
        return tensor.reshape(tensor.shape[0], HEADS, HD).transpose(1, 0, 2)

    def one_head(operands):
        query_head, key_head, value_head = operands

        def one_block(query_block):
            scores = jnp.dot(query_block, key_head.T, preferred_element_type=jnp.float32) * HD ** (-0.5)
            scores = jnp.where(allowed[None, :], scores, -jnp.inf)
            weights = jnp.exp(scores - lax.optimization_barrier(jnp.max(scores, axis=1, keepdims=True)))
            denominator = lax.optimization_barrier(jnp.sum(weights, axis=1, keepdims=True))
            return jnp.dot(weights.astype(jnp.bfloat16), value_head, preferred_element_type=jnp.float32) / denominator
        blocks = lax.map(one_block, query_head.reshape(total_q // block_len, block_len, HD))
        return blocks.reshape(total_q, HD)
    merged = lax.map(one_head, (by_head(query_rows), by_head(key_rows), by_head(value_rows)))
    return merged.transpose(1, 0, 2).reshape(total_q, HEADS * HD)

def reference(video_proj, audio_proj, video_gains, audio_gains, cross_gates, timestep, video_counts, audio_counts):
    video_query = rms_normed(video_proj[0], video_gains[0])
    video_crossq = rms_normed(video_proj[1], video_gains[1])
    video_key = rms_normed(video_proj[2], video_gains[2])
    video_value = video_proj[3]
    audio_query = rms_normed(audio_proj[0], audio_gains[0])
    audio_crossq = rms_normed(audio_proj[1], audio_gains[1])
    audio_key = rms_normed(audio_proj[2], audio_gains[2])
    audio_value = audio_proj[3]
    video_live = live_mask(video_counts, VTOK_DEV, VTOKENS)
    audio_live = live_mask(audio_counts, ATOK_DEV, ATOKENS)
    video_self = attend(video_query, video_key, video_value, video_live)
    video_cross = attend(video_crossq, audio_key, audio_value, audio_live)
    audio_self = attend(audio_query, audio_key, audio_value, audio_live)
    audio_cross = attend(audio_crossq, video_key, video_value, video_live)
    gate_rows = cross_gates[:, timestep[0], :].astype(jnp.float32)
    video_mixed = (video_self + gate_rows[0][None, :] * video_cross).astype(jnp.bfloat16)
    audio_mixed = (audio_self + gate_rows[1][None, :] * audio_cross).astype(jnp.bfloat16)
    return (video_mixed, audio_mixed)
```

```python
import math

import jax
import jax.numpy as jnp
import numpy as np
from jax import lax
from jax.experimental import pallas as pl
from jax.experimental.pallas import tpu as pltpu
from jax.sharding import Mesh
from jax.sharding import PartitionSpec as P

D = 3072
HD = 128
VTOK_DEV = 128
ATOK_DEV = 32
EPSILON = 1e-06
MASKED = -1e30

YH = 2
NY = 8
NZ = 8
GROUP = D // NY
HEADS_HERE = GROUP // HD
VROWS = 16
AROWS = 4
BLOCK = 2 * VROWS + 2 * AROWS
OUT_ROWS = 2 * (VTOK_DEV + ATOK_DEV)
STAT_ROWS = OUT_ROWS // 8
BACK_ROWS = VROWS + 8
SCORE_SCALE = HD ** (-0.5) * math.log2(math.e)
VMEM_LIMIT = 48 * 1024 * 1024


def low_rows(shape):
    return lax.broadcasted_iota(jnp.int32, shape, len(shape) - 2) % 8 < 4


def swap_halves(rows):
    return pltpu.roll(rows, 4, axis=rows.ndim - 2)


def norm_kernel(core_ref, video_ref, audio_ref, gains_ref, query_ref, keyval_ref):
    core = core_ref[0]
    first = pl.multiple_of(core * VROWS, VROWS)
    half_groups = NY // 2

    def normed(halves, gain_row, extra):
        values = [half.astype(jnp.float32) for half in halves]
        total = sum(jnp.sum(v * v, axis=1, keepdims=True) for v in values)
        inverse = lax.rsqrt(total / D + EPSILON)
        return [
            v * inverse * (gains_ref[s, gain_row : gain_row + 1, :] * extra)
            for s, v in enumerate(values)
        ]

    def spread(out_ref, row, halves):
        count = halves[0].shape[0]
        for group in range(NY):
            col = (group % half_groups) * GROUP
            out_ref[group, row : row + count, :] = halves[group // half_groups][
                :, col : col + GROUP
            ].astype(jnp.bfloat16)

    def video(array):
        return [video_ref[s, array, pl.ds(first, VROWS), :] for s in range(2)]

    def audio(array):
        return [audio_ref[s, array, :, :] for s in range(2)]

    spread(keyval_ref, 0, normed(video(2), 2, 1.0))
    spread(keyval_ref, VROWS, video(3))
    audio_key = normed(audio(2), 5, 1.0)
    audio_value = [half.astype(jnp.float32) for half in audio(3)]
    spread(
        keyval_ref,
        2 * VROWS,
        [jnp.where(core == 0, k, v) for k, v in zip(audio_key, audio_value)],
    )
    spread(query_ref, 0, normed(video(0), 0, SCORE_SCALE))
    spread(query_ref, VROWS, normed(video(1), 1, SCORE_SCALE))
    audio_self = normed(audio(0), 3, SCORE_SCALE)
    audio_cross = normed(audio(1), 4, SCORE_SCALE)
    mixed = []
    for own, other in zip(audio_self, audio_cross):
        low = low_rows(own.shape)
        mixed.append(
            jnp.where(
                core == 0,
                jnp.where(low, own, swap_halves(other)),
                jnp.where(low, swap_halves(own), other),
            )
        )
    spread(query_ref, 2 * VROWS, mixed)


def attend_kernel(query_ref, keyval_ref, video_bias_ref, audio_bias_ref, out_ref):
    x_count = query_ref.shape[0]
    z_count = keyval_ref.shape[1]
    video_keys = 2 * z_count * NY * VROWS
    audio_keys = z_count * NY * 8
    video_key = keyval_ref[:, :, :, :VROWS, :].reshape(video_keys, HD)
    video_value = keyval_ref[:, :, :, VROWS : 2 * VROWS, :].reshape(video_keys, HD)

    def audio_part(which):
        rows = keyval_ref[which, :, :, 2 * VROWS :, :].astype(jnp.float32)
        return rows.reshape(audio_keys, HD).astype(jnp.bfloat16)

    audio_key, audio_value = audio_part(0), audio_part(1)
    lane = lax.broadcasted_iota(jnp.int32, (1, 8, HD), 2)
    row = lax.broadcasted_iota(jnp.int32, (1, 8, HD), 1)
    in_row = lane // 16 == row
    field = lane % 16

    def attend(queries, key, value, bias_ref):
        scores = lax.dot_general(
            queries, key, (((1,), (1,)), ((), ())), preferred_element_type=jnp.float32
        )
        scores = scores + bias_ref[0:1, :]
        top = jnp.max(scores, axis=1, keepdims=True)
        top = top.astype(jnp.bfloat16).astype(jnp.float32)
        weights = jnp.exp2(scores - top)
        total = jnp.sum(weights, axis=1, keepdims=True)
        sums = jnp.dot(
            weights.astype(jnp.bfloat16), value, preferred_element_type=jnp.float32
        )
        high = total.astype(jnp.bfloat16).astype(jnp.float32)
        groups = top.shape[0] // 8

        def wide(column):
            return jnp.broadcast_to(column, (column.shape[0], HD)).reshape(groups, 8, HD)

        stats = jnp.where(
            field == 0,
            wide(top),
            jnp.where(field == 1, wide(high), wide(total - high)),
        )
        stats = jnp.sum(jnp.where(in_row & (field < 3), stats, 0.0), axis=1)
        return (sums / total).astype(jnp.bfloat16), stats

    audio_rows = query_ref[:, :, 2 * VROWS :, :].astype(jnp.float32)
    audio_rows = audio_rows.reshape(x_count * NY // 2, 2, 8, HD)
    even, odd = audio_rows[:, 0], audio_rows[:, 1]
    low = low_rows(even.shape)
    audio_self = jnp.where(low, even, swap_halves(odd)).reshape(-1, HD).astype(jnp.bfloat16)
    audio_cross = jnp.where(low, swap_halves(even), odd).reshape(-1, HD).astype(jnp.bfloat16)

    for x in range(x_count):
        own = slice(x * ATOK_DEV, (x + 1) * ATOK_DEV)
        video_self = query_ref[x, :, :VROWS, :].reshape(VTOK_DEV, HD)
        video_cross = query_ref[x, :, VROWS : 2 * VROWS, :].reshape(VTOK_DEV, HD)
        on_video, video_stats = attend(
            jnp.concatenate([video_self, audio_cross[own]], axis=0),
            video_key,
            video_value,
            video_bias_ref,
        )
        on_audio, audio_stats = attend(
            jnp.concatenate([video_cross, audio_self[own]], axis=0),
            audio_key,
            audio_value,
            audio_bias_ref,
        )
        tokens = VTOK_DEV + ATOK_DEV
        out_ref[x, :tokens, :] = on_video
        out_ref[x, tokens:OUT_ROWS, :] = on_audio
        out_ref[x, OUT_ROWS:, :] = jnp.concatenate(
            [video_stats, audio_stats], axis=0
        ).astype(jnp.bfloat16)


def combine_kernel(part_ref, gate_ref, out_ref):
    parts = part_ref.shape[0]
    lane = lax.broadcasted_iota(jnp.int32, (1, 8, HD), 2)
    row = lax.broadcasted_iota(jnp.int32, (1, 8, HD), 1)

    def stat(rows, number):
        picked = jnp.where(lane == row * 16 + number, rows, 0.0)
        return jnp.sum(picked.reshape(OUT_ROWS, HD), axis=1, keepdims=True)

    tops, totals = [], []
    for part in range(parts):
        rows = part_ref[part, OUT_ROWS:, :].astype(jnp.float32)
        rows = jnp.broadcast_to(rows[:, None, :], (STAT_ROWS, 8, HD))
        tops.append(stat(rows, 0))
        totals.append(stat(rows, 1) + stat(rows, 2))
    top = tops[0]
    for other in tops[1:]:
        top = jnp.maximum(top, other)
    shares = [jnp.exp2(t - top) * total for t, total in zip(tops, totals)]
    inverse = 1.0 / sum(shares)
    merged = sum(
        part_ref[part, :OUT_ROWS, :].astype(jnp.float32) * (shares[part] * inverse)
        for part in range(parts)
    )
    tokens = VTOK_DEV + ATOK_DEV
    video = merged[:VTOK_DEV] + gate_ref[0:1, :] * merged[tokens : tokens + VTOK_DEV]
    audio = merged[tokens + VTOK_DEV :] + gate_ref[1:2, :] * merged[VTOK_DEV:tokens]
    out_ref[:, :VROWS, :] = video.reshape(NY, VROWS, HD).astype(jnp.bfloat16)
    for pair in range(NY // 2):
        rows = audio[pair * 8 : pair * 8 + 8].astype(jnp.bfloat16)
        out_ref[2 * pair, VROWS:, :] = rows
        out_ref[2 * pair + 1, VROWS:, :] = rows


def place_kernel(place_ref, back_ref, video_ref, audio_ref):
    core = place_ref[0]
    odd = place_ref[1]
    half_groups = NY // 2
    for j in range(half_groups):
        group = core * half_groups + j
        cols = slice(j * GROUP, (j + 1) * GROUP)
        for s in range(2):
            video_ref[s * VROWS : (s + 1) * VROWS, cols] = back_ref[s, group, :VROWS, :]
        first, second = (back_ref[s, group, VROWS:, :].astype(jnp.float32) for s in range(2))
        low = low_rows(first.shape)
        audio_ref[:, cols] = jnp.where(
            odd == 0,
            jnp.where(low, first, swap_halves(second)),
            jnp.where(low, swap_halves(first), second),
        ).astype(jnp.bfloat16)


def whole(memory_space=pltpu.VMEM):
    return pl.BlockSpec(memory_space=memory_space)


def params():
    return pltpu.CompilerParams(vmem_limit_bytes=VMEM_LIMIT)


def shards(
    video_proj,
    audio_proj,
    video_gains,
    audio_gains,
    cross_gates,
    timestep,
    video_counts,
    audio_counts,
):
    core = lax.axis_index("tp")
    ring = ("yh", "aud")
    x_count = lax.axis_size("x")
    z_count = lax.axis_size("z")
    y_index = lax.axis_index(ring)
    gate_rows = lax.dynamic_index_in_dim(cross_gates, timestep[0], 1, keepdims=False)
    small = jnp.concatenate(
        [video_gains, audio_gains, gate_rows.astype(jnp.float32)], axis=0
    )
    video_all = lax.all_gather(video_proj, "tp", axis=0)
    audio_all = lax.all_gather(audio_proj, "tp", axis=0)
    small_all = lax.all_gather(small, "tp", axis=0)
    block = jax.ShapeDtypeStruct((NY, BLOCK, GROUP), jnp.bfloat16)
    queries, keyval = pl.pallas_call(
        norm_kernel,
        out_shape=(block, block),
        in_specs=[whole(pltpu.SMEM), whole(), whole(), whole()],
        out_specs=(whole(), whole()),
        compiler_params=params(),
        name="norm",
    )(core[None], video_all, audio_all, small_all)

    keyval = lax.all_to_all(keyval, ring, split_axis=0, concat_axis=0)
    keyval, queries = lax.optimization_barrier((keyval, queries))
    keyval = lax.all_gather(keyval, "z", axis=0)
    queries = lax.all_to_all(queries, ring, split_axis=0, concat_axis=0)
    queries = lax.all_gather(queries, "x", axis=0)
    keyval = lax.all_gather(keyval, "tp", axis=0)

    shape = (YH, x_count, z_count)
    x_index = lax.axis_index("x")

    aud_of = np.arange(NY) % (NY // YH)
    video_first = (
        aud_of[None, None, :, None] * (2 * VROWS)
        + np.arange(2)[:, None, None, None] * VROWS
        + np.arange(VROWS)[None, None, None, :]
    )
    audio_first = aud_of[None, :, None] * 8 + np.arange(8)[None, None, :]
    video_width = 2 * z_count * NY * VROWS
    audio_width = z_count * NY * 8
    here_v = lax.dynamic_index_in_dim(video_counts.reshape(shape), x_index, 1, keepdims=False)
    here_a = lax.dynamic_index_in_dim(audio_counts.reshape(shape), x_index, 1, keepdims=False)
    allow_v = jnp.repeat(here_v.T, NY // YH, axis=1)
    allow_a = jnp.repeat(here_a.T, NY // YH, axis=1)
    video_bias = jnp.where(video_first < allow_v[None, :, :, None], 0.0, MASKED)
    audio_bias = jnp.where(audio_first < allow_a[:, :, None], 0.0, MASKED)
    video_bias = video_bias.astype(jnp.float32).reshape(1, video_width)
    audio_bias = audio_bias.astype(jnp.float32).reshape(1, audio_width)

    partial = pl.pallas_call(
        attend_kernel,
        grid=(HEADS_HERE,),
        out_shape=jax.ShapeDtypeStruct(
            (x_count, OUT_ROWS + STAT_ROWS, GROUP), jnp.bfloat16
        ),
        in_specs=[
            pl.BlockSpec((x_count, NY, BLOCK, HD), lambda h: (0, 0, 0, h)),
            pl.BlockSpec((2, z_count, NY, BLOCK, HD), lambda h: (0, 0, 0, 0, h)),
            pl.BlockSpec((1, video_width), lambda h: (0, 0)),
            pl.BlockSpec((1, audio_width), lambda h: (0, 0)),
        ],
        out_specs=pl.BlockSpec((x_count, OUT_ROWS + STAT_ROWS, HD), lambda h: (0, 0, h)),
        compiler_params=params(),
        name="attend",
    )(queries, keyval, video_bias, audio_bias)

    partial = lax.all_to_all(partial, "x", split_axis=0, concat_axis=0)
    gates = lax.dynamic_slice(
        small_all,
        (y_index // (NY // 2), 6, (y_index % (NY // 2)) * GROUP),
        (1, 2, GROUP),
    )[0]
    back = pl.pallas_call(
        combine_kernel,
        grid=(HEADS_HERE,),
        out_shape=jax.ShapeDtypeStruct((NY, BACK_ROWS, GROUP), jnp.bfloat16),
        in_specs=[
            pl.BlockSpec((x_count, OUT_ROWS + STAT_ROWS, HD), lambda h: (0, 0, h)),
            pl.BlockSpec((2, HD), lambda h: (0, h)),
        ],
        out_specs=pl.BlockSpec((NY, BACK_ROWS, HD), lambda h: (0, 0, h)),
        compiler_params=params(),
        name="combine",
    )(partial, gates)
    back = lax.all_to_all(back, ring, split_axis=0, concat_axis=0)
    back = lax.all_gather(back, "tp", axis=0)
    return pl.pallas_call(
        place_kernel,
        out_shape=(
            jax.ShapeDtypeStruct((2 * VROWS, D // 2), jnp.bfloat16),
            jax.ShapeDtypeStruct((2 * AROWS, D // 2), jnp.bfloat16),
        ),
        in_specs=[whole(pltpu.SMEM), whole()],
        out_specs=(whole(), whole()),
        compiler_params=params(),
        name="place",
    )(jnp.stack([core, y_index % 2]), back)


def solution(mesh):
    vid = mesh.devices.shape[0]
    cut = (YH, vid // (YH * NZ), NZ)
    fine = Mesh(
        mesh.devices.reshape(cut + mesh.devices.shape[1:]), ("yh", "x", "z", "aud", "tp")
    )
    tokens = ("yh", "x", "z", "aud")
    in_specs = (
        P(None, tokens, "tp"),
        P(None, tokens, "tp"),
        P(None, "tp"),
        P(None, "tp"),
        P(None, None, "tp"),
        P(),
        P(),
        P(),
    )
    out_specs = (P(tokens, "tp"), P(tokens, "tp"))
    return jax.shard_map(
        shards, mesh=fine, in_specs=in_specs, out_specs=out_specs, check_vma=False
    )
```

```python
import math

import jax
import jax.numpy as jnp
import numpy as np
from jax import lax
from jax.experimental import pallas as pl
from jax.experimental.pallas import tpu as pltpu
from jax.sharding import Mesh
from jax.sharding import PartitionSpec as P

D = 3072
HD = 128
VTOK_DEV = 128
ATOK_DEV = 32
EPSILON = 1e-06
MASKED = -1e30

YH = 2
NY = 8
NZ = 8
GROUP = D // NY
HEADS_HERE = GROUP // HD
VROWS = 16
AROWS = 4
BLOCK = 2 * VROWS + 2 * AROWS
OUT_ROWS = 2 * (VTOK_DEV + ATOK_DEV)
STAT_ROWS = OUT_ROWS // 8
BACK_ROWS = VROWS + 8
AUDIO_ROW = 4 * VROWS
SMALL_ROW = AUDIO_ROW + 4 * 2 * AROWS
PACK_ROWS = SMALL_ROW + 32
KEY_STEP = 256
SCORE_SCALE = HD ** (-0.5) * math.log2(math.e)
VMEM_LIMIT = 48 * 1024 * 1024
ATTEND_VMEM = 60 * 1024 * 1024


def low_rows(shape):
    return lax.broadcasted_iota(jnp.int32, shape, len(shape) - 2) % 8 < 4


def swap_halves(rows):
    return pltpu.roll(rows, 4, axis=rows.ndim - 2)


def pack_kernel(core_ref, video_ref, audio_ref, video_gains_ref, audio_gains_ref, out_ref):
    first = pl.multiple_of((1 - core_ref[0]) * VROWS, VROWS)
    for array in range(4):
        row = array * VROWS
        out_ref[row : row + VROWS, :] = video_ref[array, pl.ds(first, VROWS), :]
        row = AUDIO_ROW + array * 8
        out_ref[row : row + 8, :] = audio_ref[array]
    gains = [video_gains_ref[...], audio_gains_ref[...]]
    rest = jnp.concatenate(gains + [jnp.zeros_like(gains[0][:2])], axis=0)
    pieces = []
    for _ in range(3):
        piece = rest.astype(jnp.bfloat16).astype(jnp.float32)
        pieces.append(piece)
        rest = rest - piece
    pieces.append(jnp.zeros_like(rest))
    out_ref[SMALL_ROW:, :] = jnp.concatenate(pieces, axis=0).astype(jnp.bfloat16)


def norm_kernel(
    core_ref,
    video_ref,
    audio_ref,
    video_gains_ref,
    audio_gains_ref,
    packed_ref,
    query_ref,
    keyval_ref,
):
    core = core_ref[0]
    at_zero = core == 0
    own_first = pl.multiple_of(core * VROWS, VROWS)
    small = packed_ref[1 - core, SMALL_ROW:, :].astype(jnp.float32)
    other_gains = small[0:8] + small[8:16] + small[16:24]
    own_gains = jnp.concatenate([video_gains_ref[...], audio_gains_ref[...]], axis=0)

    def ordered(own, other):
        return [jnp.where(at_zero, own, other), jnp.where(at_zero, other, own)]

    gains = ordered(own_gains, other_gains[:6])
    half_groups = NY // 2

    def normed(halves, gain_row, extra):
        total = sum(jnp.sum(v * v, axis=1, keepdims=True) for v in halves)
        inverse = lax.rsqrt(total / D + EPSILON)
        return [
            v * inverse * (gains[s][gain_row : gain_row + 1, :] * extra)
            for s, v in enumerate(halves)
        ]

    def spread(out_ref, row, halves):
        count = halves[0].shape[0]
        for group in range(NY):
            col = (group % half_groups) * GROUP
            out_ref[group, row : row + count, :] = halves[group // half_groups][
                :, col : col + GROUP
            ].astype(jnp.bfloat16)

    def video(array):
        first = array * VROWS
        return ordered(
            video_ref[array, pl.ds(own_first, VROWS), :].astype(jnp.float32),
            packed_ref[1 - core, first : first + VROWS, :].astype(jnp.float32),
        )

    def audio(array):
        first = AUDIO_ROW + array * 8
        return ordered(
            audio_ref[array].astype(jnp.float32),
            packed_ref[1 - core, first : first + 8, :].astype(jnp.float32),
        )

    spread(keyval_ref, 0, normed(video(2), 2, 1.0))
    spread(keyval_ref, VROWS, video(3))
    audio_key = normed(audio(2), 5, 1.0)
    audio_value = audio(3)
    spread(
        keyval_ref,
        2 * VROWS,
        [jnp.where(at_zero, k, v) for k, v in zip(audio_key, audio_value)],
    )
    spread(query_ref, 0, normed(video(0), 0, SCORE_SCALE))
    spread(query_ref, VROWS, normed(video(1), 1, SCORE_SCALE))
    audio_self = normed(audio(0), 3, SCORE_SCALE)
    audio_cross = normed(audio(1), 4, SCORE_SCALE)
    mixed = []
    for own, other in zip(audio_self, audio_cross):
        low = low_rows(own.shape)
        mixed.append(
            jnp.where(
                at_zero,
                jnp.where(low, own, swap_halves(other)),
                jnp.where(low, swap_halves(own), other),
            )
        )
    spread(query_ref, 2 * VROWS, mixed)


def attend_kernel(query_ref, keyval_ref, video_bias_ref, audio_bias_ref, out_ref):
    x_count = query_ref.shape[0]
    z_count = keyval_ref.shape[0]
    video_keys = z_count * 2 * NY * VROWS
    audio_keys = z_count * NY * 8
    video_key = keyval_ref[:, :, :, :VROWS, :].reshape(video_keys, HD)
    video_value = keyval_ref[:, :, :, VROWS : 2 * VROWS, :].reshape(video_keys, HD)

    def audio_part(which):
        rows = keyval_ref[:, which, :, 2 * VROWS :, :].astype(jnp.float32)
        return rows.reshape(audio_keys, HD).astype(jnp.bfloat16)

    audio_key, audio_value = audio_part(0), audio_part(1)
    lane = lax.broadcasted_iota(jnp.int32, (1, 8, HD), 2)
    row = lax.broadcasted_iota(jnp.int32, (1, 8, HD), 1)
    in_row = lane // 16 == row
    field = lane % 16

    def attend(queries, key, value, bias_ref):
        top = None
        for first in range(0, key.shape[0], KEY_STEP):
            keys = slice(first, first + KEY_STEP)
            scores = lax.dot_general(
                queries,
                key[keys],
                (((1,), (1,)), ((), ())),
                preferred_element_type=jnp.float32,
            )
            scores = scores + bias_ref[0:1, keys]
            here = jnp.max(scores, axis=1, keepdims=True)
            here = here.astype(jnp.bfloat16).astype(jnp.float32)
            new_top = here if top is None else jnp.maximum(top, here)
            weights = jnp.exp2(scores - new_top)
            new_total = jnp.sum(weights, axis=1, keepdims=True)
            new_sums = jnp.dot(
                weights.astype(jnp.bfloat16), value[keys], preferred_element_type=jnp.float32
            )
            if top is not None:
                keep = jnp.exp2(top - new_top)
                new_total = new_total + total * keep
                new_sums = new_sums + sums * keep
            top, total, sums = new_top, new_total, new_sums
        high = total.astype(jnp.bfloat16).astype(jnp.float32)
        groups = top.shape[0] // 8

        def wide(column):
            return jnp.broadcast_to(column, (column.shape[0], HD)).reshape(groups, 8, HD)

        stats = jnp.where(
            field == 0,
            wide(top),
            jnp.where(field == 1, wide(high), wide(total - high)),
        )
        stats = jnp.sum(jnp.where(in_row & (field < 3), stats, 0.0), axis=1)
        return (sums / total).astype(jnp.bfloat16), stats

    audio_rows = query_ref[:, :, 2 * VROWS :, :].astype(jnp.float32)
    audio_rows = audio_rows.reshape(x_count * NY // 2, 2, 8, HD)
    even, odd = audio_rows[:, 0], audio_rows[:, 1]
    low = low_rows(even.shape)
    audio_self = jnp.where(low, even, swap_halves(odd)).reshape(-1, HD).astype(jnp.bfloat16)
    audio_cross = jnp.where(low, swap_halves(even), odd).reshape(-1, HD).astype(jnp.bfloat16)
    video_self = query_ref[:, :, :VROWS, :].reshape(x_count * VTOK_DEV, HD)
    video_cross = query_ref[:, :, VROWS : 2 * VROWS, :].reshape(x_count * VTOK_DEV, HD)
    stats = []
    for kind, (video, audio, key, value, bias_ref) in enumerate(
        (
            (video_self, audio_cross, video_key, video_value, video_bias_ref),
            (video_cross, audio_self, audio_key, audio_value, audio_bias_ref),
        )
    ):
        rows, stat = attend(jnp.concatenate([video, audio], axis=0), key, value, bias_ref)
        stats.append(stat)
        start = kind * (VTOK_DEV + ATOK_DEV)
        for x in range(x_count):
            first = x * VTOK_DEV
            out_ref[x, start : start + VTOK_DEV, :] = rows[first : first + VTOK_DEV]
            first = x_count * VTOK_DEV + x * ATOK_DEV
            out_ref[x, start + VTOK_DEV : start + VTOK_DEV + ATOK_DEV, :] = rows[
                first : first + ATOK_DEV
            ]
    wide_stat, narrow_stat = VTOK_DEV // 8, ATOK_DEV // 8
    for x in range(x_count):
        picked = []
        for stat in stats:
            first = x * wide_stat
            picked.append(stat[first : first + wide_stat])
            first = x_count * wide_stat + x * narrow_stat
            picked.append(stat[first : first + narrow_stat])
        out_ref[x, OUT_ROWS:, :] = jnp.concatenate(picked, axis=0).astype(jnp.bfloat16)


def combine_kernel(part_ref, gate_ref, out_ref):
    parts = part_ref.shape[0]
    lane = lax.broadcasted_iota(jnp.int32, (1, 8, HD), 2)
    row = lax.broadcasted_iota(jnp.int32, (1, 8, HD), 1)
    in_row = lane // 16 == row
    source = lax.broadcasted_iota(jnp.int32, (HD, 2 * HD), 0) % 16
    target = lax.broadcasted_iota(jnp.int32, (HD, 2 * HD), 1) // HD
    source = jnp.where(source < 3, (source + 1) // 2, 2)
    pick = jnp.where(source == target, 1.0, 0.0).astype(jnp.bfloat16)
    tokens = VTOK_DEV + ATOK_DEV
    for head in range(HEADS_HERE):
        cols = slice(head * HD, (head + 1) * HD)
        tops, totals = [], []
        for part in range(parts):
            rows = part_ref[part, OUT_ROWS:, cols].astype(jnp.float32)
            rows = jnp.broadcast_to(rows[:, None, :], (STAT_ROWS, 8, HD))
            rows = jnp.where(in_row, rows, 0.0).reshape(OUT_ROWS, HD)
            fields = jnp.dot(
                rows.astype(jnp.bfloat16), pick, preferred_element_type=jnp.float32
            )
            tops.append(fields[:, :HD])
            totals.append(fields[:, HD:])
        top = tops[0]
        for other in tops[1:]:
            top = jnp.maximum(top, other)
        shares = [jnp.exp2(t - top) * total for t, total in zip(tops, totals)]
        inverse = 1.0 / sum(shares)
        merged = sum(
            part_ref[part, :OUT_ROWS, cols].astype(jnp.float32) * (shares[part] * inverse)
            for part in range(parts)
        )
        video = merged[:VTOK_DEV] + gate_ref[0:1, cols] * merged[tokens : tokens + VTOK_DEV]
        audio = merged[tokens + VTOK_DEV :] + gate_ref[1:2, cols] * merged[VTOK_DEV:tokens]
        out_ref[:, :VROWS, cols] = video.reshape(NY, VROWS, HD).astype(jnp.bfloat16)
        for pair in range(NY // 2):
            rows = audio[pair * 8 : pair * 8 + 8].astype(jnp.bfloat16)
            out_ref[2 * pair, VROWS:, cols] = rows
            out_ref[2 * pair + 1, VROWS:, cols] = rows


def place_kernel(place_ref, back_ref, video_ref, audio_ref):
    core = place_ref[0]
    odd = place_ref[1]
    half_groups = NY // 2
    for j in range(half_groups):
        group = core * half_groups + j
        cols = slice(j * GROUP, (j + 1) * GROUP)
        for s in range(2):
            video_ref[s * VROWS : (s + 1) * VROWS, cols] = back_ref[s, group, :VROWS, :]
        first, second = (back_ref[s, group, VROWS:, :].astype(jnp.float32) for s in range(2))
        low = low_rows(first.shape)
        audio_ref[:, cols] = jnp.where(
            odd == 0,
            jnp.where(low, first, swap_halves(second)),
            jnp.where(low, swap_halves(first), second),
        ).astype(jnp.bfloat16)


def whole(memory_space=pltpu.VMEM):
    return pl.BlockSpec(memory_space=memory_space)


def params():
    return pltpu.CompilerParams(vmem_limit_bytes=VMEM_LIMIT)


def shards(
    video_proj,
    audio_proj,
    video_gains,
    audio_gains,
    cross_gates,
    timestep,
    video_counts,
    audio_counts,
):
    core = lax.axis_index("tp")
    ring = ("yh", "aud")
    x_count = lax.axis_size("x")
    z_count = lax.axis_size("z")
    y_index = lax.axis_index(ring)
    packed = pl.pallas_call(
        pack_kernel,
        grid=(1,),
        out_shape=jax.ShapeDtypeStruct((PACK_ROWS, D // 2), jnp.bfloat16),
        in_specs=[
            whole(pltpu.SMEM),
            pl.BlockSpec(video_proj.shape, lambda i: (0, 0, 0)),
            pl.BlockSpec(audio_proj.shape, lambda i: (0, 0, 0)),
            pl.BlockSpec(video_gains.shape, lambda i: (0, 0)),
            pl.BlockSpec(audio_gains.shape, lambda i: (0, 0)),
        ],
        out_specs=pl.BlockSpec((PACK_ROWS, D // 2), lambda i: (0, 0)),
        compiler_params=pltpu.CompilerParams(vmem_limit_bytes=ATTEND_VMEM),
        name="pack",
    )(core[None], video_proj, audio_proj, video_gains, audio_gains)
    packed = lax.all_gather(packed, "tp", axis=0)
    block = jax.ShapeDtypeStruct((NY, BLOCK, GROUP), jnp.bfloat16)
    queries, keyval = pl.pallas_call(
        norm_kernel,
        out_shape=(block, block),
        in_specs=[whole(pltpu.SMEM)] + [whole()] * 5,
        out_specs=(whole(), whole()),
        compiler_params=params(),
        name="norm",
    )(core[None], video_proj, audio_proj, video_gains, audio_gains, packed)

    keyval = lax.all_to_all(keyval, ring, split_axis=0, concat_axis=0)
    keyval, queries = lax.optimization_barrier((keyval, queries))
    keyval = lax.all_gather(keyval, ("z", "tp"), axis=0)
    keyval = keyval.reshape(z_count, 2, NY, BLOCK, GROUP)
    queries = lax.all_to_all(queries, ring, split_axis=0, concat_axis=0)
    queries = lax.all_gather(queries, "x", axis=0)

    shape = (YH, x_count, z_count)
    x_index = lax.axis_index("x")

    aud_of = np.arange(NY) % (NY // YH)
    video_first = (
        aud_of[None, None, :, None] * (2 * VROWS)
        + np.arange(2)[None, :, None, None] * VROWS
        + np.arange(VROWS)[None, None, None, :]
    )
    audio_first = aud_of[None, :, None] * 8 + np.arange(8)[None, None, :]
    video_width = z_count * 2 * NY * VROWS
    audio_width = z_count * NY * 8

    def allowed(counts):
        here = lax.dynamic_index_in_dim(counts.reshape(shape), x_index, 1, keepdims=False)
        return jnp.repeat(here.T, NY // YH, axis=1)

    video_bias = jnp.where(
        video_first < allowed(video_counts)[:, None, :, None], 0.0, MASKED
    )
    audio_bias = jnp.where(audio_first < allowed(audio_counts)[:, :, None], 0.0, MASKED)
    video_bias = video_bias.astype(jnp.float32).reshape(1, video_width)
    audio_bias = audio_bias.astype(jnp.float32).reshape(1, audio_width)
    queries, video_bias, audio_bias, step = lax.optimization_barrier(
        (queries, video_bias, audio_bias, timestep)
    )
    gates = lax.dynamic_index_in_dim(cross_gates, step[0], 1, keepdims=False)
    gates = lax.all_gather(gates, "tp", axis=0)
    gates = lax.dynamic_slice(
        gates,
        (y_index // (NY // 2), 0, (y_index % (NY // 2)) * GROUP),
        (1, 2, GROUP),
    )[0].astype(jnp.float32)
    queries, gates = lax.optimization_barrier((queries, gates))

    partial = pl.pallas_call(
        attend_kernel,
        grid=(HEADS_HERE,),
        out_shape=jax.ShapeDtypeStruct(
            (x_count, OUT_ROWS + STAT_ROWS, GROUP), jnp.bfloat16
        ),
        in_specs=[
            pl.BlockSpec((x_count, NY, BLOCK, HD), lambda h: (0, 0, 0, h)),
            pl.BlockSpec((z_count, 2, NY, BLOCK, HD), lambda h: (0, 0, 0, 0, h)),
            pl.BlockSpec((1, video_width), lambda h: (0, 0)),
            pl.BlockSpec((1, audio_width), lambda h: (0, 0)),
        ],
        out_specs=pl.BlockSpec((x_count, OUT_ROWS + STAT_ROWS, HD), lambda h: (0, 0, h)),
        compiler_params=pltpu.CompilerParams(vmem_limit_bytes=ATTEND_VMEM),
        name="attend",
    )(queries, keyval, video_bias, audio_bias)

    partial = lax.all_to_all(partial, "x", split_axis=0, concat_axis=0)
    back = pl.pallas_call(
        combine_kernel,
        out_shape=jax.ShapeDtypeStruct((NY, BACK_ROWS, GROUP), jnp.bfloat16),
        in_specs=[whole(), whole()],
        out_specs=whole(),
        compiler_params=params(),
        name="combine",
    )(partial, gates)
    back = lax.all_to_all(back, ring, split_axis=0, concat_axis=0)
    back = lax.all_gather(back, "tp", axis=0)
    return pl.pallas_call(
        place_kernel,
        out_shape=(
            jax.ShapeDtypeStruct((2 * VROWS, D // 2), jnp.bfloat16),
            jax.ShapeDtypeStruct((2 * AROWS, D // 2), jnp.bfloat16),
        ),
        in_specs=[whole(pltpu.SMEM), whole()],
        out_specs=(whole(), whole()),
        compiler_params=params(),
        name="place",
    )(jnp.stack([core, y_index % 2]), back)


def solution(mesh):
    vid = mesh.devices.shape[0]
    cut = (YH, vid // (YH * NZ), NZ)
    fine = Mesh(
        mesh.devices.reshape(cut + mesh.devices.shape[1:]), ("yh", "x", "z", "aud", "tp")
    )
    tokens = ("yh", "x", "z", "aud")
    in_specs = (
        P(None, tokens, "tp"),
        P(None, tokens, "tp"),
        P(None, "tp"),
        P(None, "tp"),
        P(None, None, "tp"),
        P(),
        P(),
        P(),
    )
    out_specs = (P(tokens, "tp"), P(tokens, "tp"))
    return jax.shard_map(
        shards, mesh=fine, in_specs=in_specs, out_specs=out_specs, check_vma=False
    )
```

```python
import functools
import math

import jax
import jax.numpy as jnp
import numpy as np
from jax import lax
from jax.experimental import pallas as pl
from jax.experimental.pallas import tpu as pltpu
from jax.sharding import Mesh
from jax.sharding import PartitionSpec as P

D = 3072
HD = 128
VTOK_DEV = 128
ATOK_DEV = 32
EPSILON = 1e-06
MASKED = -1e30

YH = 2
NY = 8
ZP = 2
ZQ = 4
GROUP = D // NY
HEADS_HERE = GROUP // HD
VROWS = 16
AROWS = 4
BLOCK = 2 * VROWS + 2 * AROWS
OUT_ROWS = 2 * (VTOK_DEV + ATOK_DEV)
STAT_ROWS = OUT_ROWS // 8
BACK_ROWS = VROWS + 8
AUDIO_ROW = 4 * VROWS
SMALL_ROW = AUDIO_ROW + 4 * 2 * AROWS
PACK_ROWS = SMALL_ROW + 32
KEY_STEP = 256
SCORE_SCALE = HD ** (-0.5) * math.log2(math.e)
VMEM_LIMIT = 48 * 1024 * 1024
PACK_VMEM = 60 * 1024 * 1024


def low_rows(shape):
    return lax.broadcasted_iota(jnp.int32, shape, len(shape) - 2) % 8 < 4


def swap_halves(rows):
    return pltpu.roll(rows, 4, axis=rows.ndim - 2)


def pack_kernel(core_ref, video_ref, audio_ref, video_gains_ref, audio_gains_ref, out_ref):
    first = pl.multiple_of((1 - core_ref[0]) * VROWS, VROWS)
    for array in range(4):
        row = array * VROWS
        out_ref[row : row + VROWS, :] = video_ref[array, pl.ds(first, VROWS), :]
        row = AUDIO_ROW + array * 8
        out_ref[row : row + 8, :] = audio_ref[array]
    gains = [video_gains_ref[...], audio_gains_ref[...]]
    rest = jnp.concatenate(gains + [jnp.zeros_like(gains[0][:2])], axis=0)
    pieces = []
    for _ in range(3):
        piece = rest.astype(jnp.bfloat16).astype(jnp.float32)
        pieces.append(piece)
        rest = rest - piece
    pieces.append(jnp.zeros_like(rest))
    out_ref[SMALL_ROW:, :] = jnp.concatenate(pieces, axis=0).astype(jnp.bfloat16)


def norm_kernel(
    for_queries,
    core_ref,
    video_ref,
    audio_ref,
    video_gains_ref,
    audio_gains_ref,
    packed_ref,
    out_ref,
):
    core = core_ref[0]
    at_zero = core == 0
    own_first = pl.multiple_of(core * VROWS, VROWS)
    small = packed_ref[1 - core, SMALL_ROW:, :].astype(jnp.float32)
    other_gains = small[0:8] + small[8:16] + small[16:24]
    own_gains = jnp.concatenate([video_gains_ref[...], audio_gains_ref[...]], axis=0)

    def ordered(own, other):
        return [jnp.where(at_zero, own, other), jnp.where(at_zero, other, own)]

    gains = ordered(own_gains, other_gains[:6])
    half_groups = NY // 2

    def normed(halves, gain_row, extra):
        total = sum(jnp.sum(v * v, axis=1, keepdims=True) for v in halves)
        inverse = lax.rsqrt(total / D + EPSILON)
        return [
            v * inverse * (gains[s][gain_row : gain_row + 1, :] * extra)
            for s, v in enumerate(halves)
        ]

    def spread(row, halves):
        count = halves[0].shape[0]
        for group in range(NY):
            col = (group % half_groups) * GROUP
            rows = halves[group // half_groups][:, col : col + GROUP].astype(jnp.bfloat16)
            if for_queries:
                out_ref[group, row : row + count, :] = rows
            else:
                yh, aud = divmod(group, NY // YH)
                for zq in range(out_ref.shape[1]):
                    out_ref[yh, zq, aud, row : row + count, :] = rows

    def video(array):
        first = array * VROWS
        return ordered(
            video_ref[array, pl.ds(own_first, VROWS), :].astype(jnp.float32),
            packed_ref[1 - core, first : first + VROWS, :].astype(jnp.float32),
        )

    def audio(array):
        first = AUDIO_ROW + array * 8
        return ordered(
            audio_ref[array].astype(jnp.float32),
            packed_ref[1 - core, first : first + 8, :].astype(jnp.float32),
        )

    if not for_queries:
        spread(0, normed(video(2), 2, 1.0))
        spread(VROWS, video(3))
        audio_key = normed(audio(2), 5, 1.0)
        audio_value = audio(3)
        spread(
            2 * VROWS,
            [jnp.where(at_zero, k, v) for k, v in zip(audio_key, audio_value)],
        )
        return
    spread(0, normed(video(0), 0, SCORE_SCALE))
    spread(VROWS, normed(video(1), 1, SCORE_SCALE))
    audio_self = normed(audio(0), 3, SCORE_SCALE)
    audio_cross = normed(audio(1), 4, SCORE_SCALE)
    mixed = []
    for own, other in zip(audio_self, audio_cross):
        low = low_rows(own.shape)
        mixed.append(
            jnp.where(
                at_zero,
                jnp.where(low, own, swap_halves(other)),
                jnp.where(low, swap_halves(own), other),
            )
        )
    spread(2 * VROWS, mixed)


def attend_kernel(parities, begins, ends, core_ref, query_ref, *refs):
    x_count = query_ref.shape[0]
    keyval_refs = refs[: 2 * parities]
    video_bias_ref, audio_bias_ref, *rest = refs[2 * parities :]
    holds_keys = core_ref[0] == 0

    def rows_of(ref, first, last):
        rows = ref[:, :, :, first:last, :]
        if last - first == 8:
            rows = rows.astype(jnp.float32)
        return rows.reshape(-1, HD)

    video_pieces, audio_pieces = [], []
    for own, other in zip(keyval_refs[::2], keyval_refs[1::2]):
        for ref in (own, other):
            key = rows_of(ref, 0, VROWS)
            value = rows_of(ref, VROWS, 2 * VROWS)
            for first in range(0, key.shape[0], KEY_STEP):
                keys = slice(first, first + KEY_STEP)
                video_pieces.append((key[keys], value[keys]))
        own, other = (rows_of(ref, 2 * VROWS, BLOCK) for ref in (own, other))
        audio_pieces.append(
            (
                jnp.where(holds_keys, own, other).astype(jnp.bfloat16),
                jnp.where(holds_keys, other, own).astype(jnp.bfloat16),
            )
        )
    lane = lax.broadcasted_iota(jnp.int32, (1, 8, HD), 2)
    row = lax.broadcasted_iota(jnp.int32, (1, 8, HD), 1)
    in_row = lane // 16 == row
    field = lane % 16

    def attend(queries, pieces, bias_ref, state):
        first = 0
        for key, value in pieces:
            keys = slice(first, first + key.shape[0])
            first = keys.stop
            scores = lax.dot_general(
                queries, key, (((1,), (1,)), ((), ())), preferred_element_type=jnp.float32
            )
            scores = scores + bias_ref[0:1, keys]
            top = jnp.max(scores, axis=1, keepdims=True)
            top = top.astype(jnp.bfloat16).astype(jnp.float32)
            if state is not None:
                top = jnp.maximum(top, state[0])
            weights = jnp.exp2(scores - top)
            total = jnp.sum(weights, axis=1, keepdims=True)
            sums = jnp.dot(
                weights.astype(jnp.bfloat16), value, preferred_element_type=jnp.float32
            )
            if state is not None:
                keep = jnp.exp2(state[0] - top)
                total = total + state[1] * keep
                sums = sums + state[2] * keep
            state = top, total, sums
        return state

    def finish(top, total, sums):
        high = total.astype(jnp.bfloat16).astype(jnp.float32)
        groups = top.shape[0] // 8

        def wide(column):
            return jnp.broadcast_to(column, (column.shape[0], HD)).reshape(groups, 8, HD)

        stats = jnp.where(
            field == 0,
            wide(top),
            jnp.where(field == 1, wide(high), wide(total - high)),
        )
        stats = jnp.sum(jnp.where(in_row & (field < 3), stats, 0.0), axis=1)
        return (sums / total).astype(jnp.bfloat16), stats

    audio_rows = query_ref[:, :, 2 * VROWS :, :].astype(jnp.float32)
    audio_rows = audio_rows.reshape(x_count * NY // 2, 2, 8, HD)
    even, odd = audio_rows[:, 0], audio_rows[:, 1]
    low = low_rows(even.shape)
    audio_self = jnp.where(low, even, swap_halves(odd)).reshape(-1, HD).astype(jnp.bfloat16)
    audio_cross = jnp.where(low, swap_halves(even), odd).reshape(-1, HD).astype(jnp.bfloat16)
    video_self = query_ref[:, :, :VROWS, :].reshape(x_count * VTOK_DEV, HD)
    video_cross = query_ref[:, :, VROWS : 2 * VROWS, :].reshape(x_count * VTOK_DEV, HD)
    queries = (
        jnp.concatenate([video_self, audio_cross], axis=0),
        jnp.concatenate([video_cross, audio_self], axis=0),
    )
    pieces = (video_pieces, audio_pieces)
    biases = (video_bias_ref, audio_bias_ref)
    count = queries[0].shape[0]
    stats = []
    for kind in range(2):
        rows = slice(kind * count, (kind + 1) * count)
        state = attend(queries[kind], pieces[kind], biases[kind], None)
        top, total, sums = state
        if not ends:
            sums_ref, level_ref = rest
            sums_ref[rows, :] = (sums / total).astype(jnp.bfloat16)
            level_ref[rows, :] = jnp.broadcast_to(top + jnp.log2(total), (count, HD))
            continue
        if not begins:
            old_sums_ref, old_level_ref, _ = rest
            old_level = old_level_ref[rows, :]
            new_top = jnp.maximum(top, old_level.astype(jnp.bfloat16).astype(jnp.float32))
            keep, old_share = jnp.exp2(top - new_top), jnp.exp2(old_level - new_top)
            total = total * keep + old_share
            sums = sums * keep + old_sums_ref[rows, :].astype(jnp.float32) * old_share
            state = new_top, total, sums
        out_ref = rest[-1]
        rows, stat = finish(*state)
        stats.append(stat)
        start = kind * (VTOK_DEV + ATOK_DEV)
        for x in range(x_count):
            first = x * VTOK_DEV
            out_ref[x, start : start + VTOK_DEV, :] = rows[first : first + VTOK_DEV]
            first = x_count * VTOK_DEV + x * ATOK_DEV
            out_ref[x, start + VTOK_DEV : start + VTOK_DEV + ATOK_DEV, :] = rows[
                first : first + ATOK_DEV
            ]
    if not ends:
        return
    wide_stat, narrow_stat = VTOK_DEV // 8, ATOK_DEV // 8
    for x in range(x_count):
        picked = []
        for stat in stats:
            first = x * wide_stat
            picked.append(stat[first : first + wide_stat])
            first = x_count * wide_stat + x * narrow_stat
            picked.append(stat[first : first + narrow_stat])
        out_ref[x, OUT_ROWS:, :] = jnp.concatenate(picked, axis=0).astype(jnp.bfloat16)


def combine_kernel(part_ref, gate_ref, out_ref):
    parts = part_ref.shape[0]
    lane = lax.broadcasted_iota(jnp.int32, (1, 8, HD), 2)
    row = lax.broadcasted_iota(jnp.int32, (1, 8, HD), 1)
    in_row = lane // 16 == row
    source = lax.broadcasted_iota(jnp.int32, (HD, 2 * HD), 0) % 16
    target = lax.broadcasted_iota(jnp.int32, (HD, 2 * HD), 1) // HD
    source = jnp.where(source < 3, (source + 1) // 2, 2)
    pick = jnp.where(source == target, 1.0, 0.0).astype(jnp.bfloat16)
    tokens = VTOK_DEV + ATOK_DEV
    for head in range(HEADS_HERE):
        cols = slice(head * HD, (head + 1) * HD)
        tops, totals = [], []
        for part in range(parts):
            rows = part_ref[part, OUT_ROWS:, cols].astype(jnp.float32)
            rows = jnp.broadcast_to(rows[:, None, :], (STAT_ROWS, 8, HD))
            rows = jnp.where(in_row, rows, 0.0).reshape(OUT_ROWS, HD)
            fields = jnp.dot(
                rows.astype(jnp.bfloat16), pick, preferred_element_type=jnp.float32
            )
            tops.append(fields[:, :HD])
            totals.append(fields[:, HD:])
        top = tops[0]
        for other in tops[1:]:
            top = jnp.maximum(top, other)
        shares = [jnp.exp2(t - top) * total for t, total in zip(tops, totals)]
        inverse = 1.0 / sum(shares)
        merged = sum(
            part_ref[part, :OUT_ROWS, cols].astype(jnp.float32) * (shares[part] * inverse)
            for part in range(parts)
        )
        video = merged[:VTOK_DEV] + gate_ref[0:1, cols] * merged[tokens : tokens + VTOK_DEV]
        audio = merged[tokens + VTOK_DEV :] + gate_ref[1:2, cols] * merged[VTOK_DEV:tokens]
        out_ref[:, :VROWS, cols] = video.reshape(NY, VROWS, HD).astype(jnp.bfloat16)
        for pair in range(NY // 2):
            rows = audio[pair * 8 : pair * 8 + 8].astype(jnp.bfloat16)
            out_ref[2 * pair, VROWS:, cols] = rows
            out_ref[2 * pair + 1, VROWS:, cols] = rows


def place_kernel(place_ref, back_ref, video_ref, audio_ref):
    core = place_ref[0]
    odd = place_ref[1]
    half_groups = NY // 2
    for j in range(half_groups):
        group = core * half_groups + j
        cols = slice(j * GROUP, (j + 1) * GROUP)
        for s in range(2):
            video_ref[s * VROWS : (s + 1) * VROWS, cols] = back_ref[s, group, :VROWS, :]
        first, second = (back_ref[s, group, VROWS:, :].astype(jnp.float32) for s in range(2))
        low = low_rows(first.shape)
        audio_ref[:, cols] = jnp.where(
            odd == 0,
            jnp.where(low, first, swap_halves(second)),
            jnp.where(low, swap_halves(first), second),
        ).astype(jnp.bfloat16)


def whole(memory_space=pltpu.VMEM):
    return pl.BlockSpec(memory_space=memory_space)


def params():
    return pltpu.CompilerParams(vmem_limit_bytes=VMEM_LIMIT)


def shards(
    video_proj,
    audio_proj,
    video_gains,
    audio_gains,
    cross_gates,
    timestep,
    video_counts,
    audio_counts,
):
    core = lax.axis_index("tp")
    ring = ("yh", "aud")
    x_count = lax.axis_size("x")
    zq_count = lax.axis_size("zq")
    z_parity = lax.axis_index("zp")
    y_index = lax.axis_index(ring)
    packed = pl.pallas_call(
        pack_kernel,
        grid=(1,),
        out_shape=jax.ShapeDtypeStruct((PACK_ROWS, D // 2), jnp.bfloat16),
        in_specs=[
            whole(pltpu.SMEM),
            pl.BlockSpec(video_proj.shape, lambda i: (0, 0, 0)),
            pl.BlockSpec(audio_proj.shape, lambda i: (0, 0, 0)),
            pl.BlockSpec(video_gains.shape, lambda i: (0, 0)),
            pl.BlockSpec(audio_gains.shape, lambda i: (0, 0)),
        ],
        out_specs=pl.BlockSpec((PACK_ROWS, D // 2), lambda i: (0, 0)),
        compiler_params=pltpu.CompilerParams(vmem_limit_bytes=PACK_VMEM),
        name="pack",
    )(core[None], video_proj, audio_proj, video_gains, audio_gains)
    packed = lax.all_gather(packed, "tp", axis=0)
    def norm(for_queries, shape):
        return pl.pallas_call(
            functools.partial(norm_kernel, for_queries),
            out_shape=jax.ShapeDtypeStruct(shape + (BLOCK, GROUP), jnp.bfloat16),
            in_specs=[whole(pltpu.SMEM)] + [whole()] * 5,
            out_specs=whole(),
            compiler_params=params(),
            name="norm_queries" if for_queries else "norm_keys",
        )(core[None], video_proj, audio_proj, video_gains, audio_gains, packed)

    queries = norm(True, (NY,))
    keyval = norm(False, (YH, zq_count, NY // YH))

    full_shape = keyval.shape
    keyval = keyval.reshape((YH * zq_count * (NY // YH),) + full_shape[3:])
    keyval = lax.all_to_all(keyval, ("yh", "zq", "aud"), split_axis=0, concat_axis=0)
    queries = lax.all_to_all(queries, ring, split_axis=0, concat_axis=0)
    queries = lax.all_gather(queries, "x", axis=0)

    x_index = lax.axis_index("x")
    aud_first = np.arange(NY // YH)
    parities = jnp.stack([z_parity, 1 - z_parity])
    halves = jnp.stack([core, 1 - core])

    def allowed(counts):
        here = counts.reshape(YH, x_count, zq_count, ZP)
        here = lax.dynamic_index_in_dim(here, x_index, 1, keepdims=False)
        here = jnp.moveaxis(here, 2, 0)
        return jnp.where(z_parity == 0, here, here[::-1])

    def bias(live):
        return jnp.where(live, 0.0, MASKED).astype(jnp.float32).reshape(1, -1)

    video_first = (
        aud_first[None, :, None] * (2 * VROWS)
        + halves[:, None, None] * VROWS
        + np.arange(VROWS)[None, None, :]
    )
    audio_first = aud_first[:, None] * 8 + np.arange(8)[None, :]
    allowed_video, allowed_audio = allowed(video_counts), allowed(audio_counts)
    biases = [
        (
            bias(video_first[:, None, None] < allowed_video[parity][None, :, :, None, None]),
            bias(audio_first < allowed_audio[parity][..., None, None]),
        )
        for parity in range(ZP)
    ]
    places = jnp.stack([core, y_index % 2])
    gates = lax.dynamic_index_in_dim(cross_gates, timestep[0], 1, keepdims=False)
    gates, packed = lax.optimization_barrier((gates, packed))
    gates = lax.all_gather(gates, "tp", axis=0)
    gates = lax.dynamic_slice(
        gates,
        (y_index // (NY // 2), 0, (y_index % (NY // 2)) * GROUP),
        (1, 2, GROUP),
    )[0].astype(jnp.float32)
    queries, gates, biases, keyval, places = lax.optimization_barrier(
        (queries, gates, biases, keyval, places)
    )

    ways = [
        (z * 2 + c, (z + 1 - 2 * c) % (ZP * zq_count) * 2 + c)
        for z in range(ZP * zq_count)
        for c in range(2)
    ]
    swap = [(0, 1), (1, 0)]
    far = lax.ppermute(keyval, ("zq", "zp", "tp"), ways)
    keyval_other = lax.ppermute(keyval, "tp", swap)
    near = [keyval.reshape(full_shape), keyval_other.reshape(full_shape)]

    def attend(keyvals, video_bias, audio_bias, state, ends):
        parities = len(keyvals) // 2
        rows = 2 * x_count * (VTOK_DEV + ATOK_DEV)
        state_spec = pl.BlockSpec((rows, HD), lambda h: (0, h))
        if ends:
            out_shape = jax.ShapeDtypeStruct(
                (x_count, OUT_ROWS + STAT_ROWS, GROUP), jnp.bfloat16
            )
            out_specs = pl.BlockSpec(
                (x_count, OUT_ROWS + STAT_ROWS, HD), lambda h: (0, 0, h)
            )
        else:
            out_shape = tuple(
                jax.ShapeDtypeStruct((rows, GROUP), dtype)
                for dtype in (jnp.bfloat16, jnp.float32)
            )
            out_specs = (state_spec,) * 2
        keyval_spec = pl.BlockSpec(full_shape[:-1] + (HD,), lambda h: (0, 0, 0, 0, h))
        return pl.pallas_call(
            functools.partial(attend_kernel, parities, not state, ends),
            grid=(HEADS_HERE,),
            out_shape=out_shape,
            in_specs=[
                whole(pltpu.SMEM),
                pl.BlockSpec((x_count, NY, BLOCK, HD), lambda h: (0, 0, 0, h)),
                *[keyval_spec] * len(keyvals),
                pl.BlockSpec(video_bias.shape, lambda h: (0, 0)),
                pl.BlockSpec(audio_bias.shape, lambda h: (0, 0)),
                *[state_spec] * len(state),
            ],
            out_specs=out_specs,
            compiler_params=params(),
            name="attend_near" if not ends else "attend",
        )(core[None], queries, *keyvals, video_bias, audio_bias, *state)

    state = attend(near, *biases[0], (), False)
    far, *state = lax.optimization_barrier((far, *state))
    far_other = lax.ppermute(far, "tp", swap)
    far = [far.reshape(full_shape), far_other.reshape(full_shape)]
    partial = attend(far, *biases[1], state, True)
    partial = lax.all_to_all(partial, "x", split_axis=0, concat_axis=0)
    back = pl.pallas_call(
        combine_kernel,
        out_shape=jax.ShapeDtypeStruct((NY, BACK_ROWS, GROUP), jnp.bfloat16),
        in_specs=[whole(), whole()],
        out_specs=whole(),
        compiler_params=params(),
        name="combine",
    )(partial, gates)
    back = lax.all_to_all(back, ring, split_axis=0, concat_axis=0)
    back = lax.all_gather(back, "tp", axis=0)
    return pl.pallas_call(
        place_kernel,
        out_shape=(
            jax.ShapeDtypeStruct((2 * VROWS, D // 2), jnp.bfloat16),
            jax.ShapeDtypeStruct((2 * AROWS, D // 2), jnp.bfloat16),
        ),
        in_specs=[whole(pltpu.SMEM), whole()],
        out_specs=(whole(), whole()),
        compiler_params=params(),
        name="place",
    )(places, back)


def solution(mesh):
    vid = mesh.devices.shape[0]
    cut = (YH, vid // (YH * ZQ * ZP), ZQ, ZP)
    axes = ("yh", "x", "zq", "zp", "aud", "tp")
    fine = Mesh(mesh.devices.reshape(cut + mesh.devices.shape[1:]), axes)
    tokens = axes[:-1]
    in_specs = (
        P(None, tokens, "tp"),
        P(None, tokens, "tp"),
        P(None, "tp"),
        P(None, "tp"),
        P(None, None, "tp"),
        P(),
        P(),
        P(),
    )
    out_specs = (P(tokens, "tp"), P(tokens, "tp"))
    return jax.shard_map(
        shards, mesh=fine, in_specs=in_specs, out_specs=out_specs, check_vma=False
    )
```

```python
import functools
import math

import jax
import jax.numpy as jnp
import numpy as np
from jax import lax
from jax.experimental import pallas as pl
from jax.experimental.pallas import tpu as pltpu
from jax.sharding import Mesh
from jax.sharding import PartitionSpec as P

D = 3072
HD = 128
VTOK_DEV = 128
ATOK_DEV = 32
EPSILON = 1e-06
MASKED = -1e30

YH = 2
NY = 8
ZP = 2
ZQ = 4
GROUP = D // NY
HEADS_HERE = GROUP // HD
VROWS = 16
AROWS = 4
BLOCK = 2 * VROWS + 2 * AROWS
OUT_ROWS = 2 * (VTOK_DEV + ATOK_DEV)
STAT_ROWS = OUT_ROWS // 8
BACK_ROWS = VROWS + 8
AUDIO_ROW = 4 * VROWS
SMALL_ROW = AUDIO_ROW + 4 * 2 * AROWS
PACK_ROWS = SMALL_ROW + 32
KEY_STEP = 256
SCORE_SCALE = HD ** (-0.5) * math.log2(math.e)
VMEM_LIMIT = 48 * 1024 * 1024
PACK_VMEM = 60 * 1024 * 1024


def low_rows(shape):
    return lax.broadcasted_iota(jnp.int32, shape, len(shape) - 2) % 8 < 4


def swap_halves(rows):
    return pltpu.roll(rows, 4, axis=rows.ndim - 2)


def pack_kernel(core_ref, video_ref, audio_ref, video_gains_ref, audio_gains_ref, out_ref):
    first = pl.multiple_of((1 - core_ref[0]) * VROWS, VROWS)
    for array in range(4):
        row = array * VROWS
        out_ref[row : row + VROWS, :] = video_ref[array, pl.ds(first, VROWS), :]
        row = AUDIO_ROW + array * 8
        out_ref[row : row + 8, :] = audio_ref[array]
    gains = [video_gains_ref[...], audio_gains_ref[...]]
    rest = jnp.concatenate(gains + [jnp.zeros_like(gains[0][:2])], axis=0)
    pieces = []
    for _ in range(3):
        piece = rest.astype(jnp.bfloat16).astype(jnp.float32)
        pieces.append(piece)
        rest = rest - piece
    pieces.append(jnp.zeros_like(rest))
    out_ref[SMALL_ROW:, :] = jnp.concatenate(pieces, axis=0).astype(jnp.bfloat16)


def norm_kernel(
    core_ref,
    video_ref,
    audio_ref,
    video_gains_ref,
    audio_gains_ref,
    packed_ref,
    out_ref,
):
    core = core_ref[0]
    at_zero = core == 0
    own_first = pl.multiple_of(core * VROWS, VROWS)
    small = packed_ref[1 - core, SMALL_ROW:, :].astype(jnp.float32)
    other_gains = small[0:8] + small[8:16] + small[16:24]
    own_gains = jnp.concatenate([video_gains_ref[...], audio_gains_ref[...]], axis=0)

    def ordered(own, other):
        return [jnp.where(at_zero, own, other), jnp.where(at_zero, other, own)]

    gains = ordered(own_gains, other_gains[:6])
    half_groups = NY // 2

    def normed(halves, gain_row, extra):
        total = sum(jnp.sum(v * v, axis=1, keepdims=True) for v in halves)
        inverse = lax.rsqrt(total / D + EPSILON)
        return [
            v * inverse * (gains[s][gain_row : gain_row + 1, :] * extra)
            for s, v in enumerate(halves)
        ]

    def spread(row, halves):
        count = halves[0].shape[0]
        for group in range(NY):
            col = (group % half_groups) * GROUP
            out_ref[group, row : row + count, :] = halves[group // half_groups][
                :, col : col + GROUP
            ].astype(jnp.bfloat16)

    def video(array):
        first = array * VROWS
        return ordered(
            video_ref[array, pl.ds(own_first, VROWS), :].astype(jnp.float32),
            packed_ref[1 - core, first : first + VROWS, :].astype(jnp.float32),
        )

    def audio(array):
        first = AUDIO_ROW + array * 8
        return ordered(
            audio_ref[array].astype(jnp.float32),
            packed_ref[1 - core, first : first + 8, :].astype(jnp.float32),
        )

    spread(0, normed(video(2), 2, 1.0))
    spread(VROWS, video(3))
    audio_key = normed(audio(2), 5, 1.0)
    audio_value = audio(3)
    spread(
        2 * VROWS,
        [jnp.where(at_zero, k, v) for k, v in zip(audio_key, audio_value)],
    )
    spread(BLOCK, normed(video(0), 0, SCORE_SCALE))
    spread(BLOCK + VROWS, normed(video(1), 1, SCORE_SCALE))
    audio_self = normed(audio(0), 3, SCORE_SCALE)
    audio_cross = normed(audio(1), 4, SCORE_SCALE)
    mixed = []
    for own, other in zip(audio_self, audio_cross):
        low = low_rows(own.shape)
        mixed.append(
            jnp.where(
                at_zero,
                jnp.where(low, own, swap_halves(other)),
                jnp.where(low, swap_halves(own), other),
            )
        )
    spread(BLOCK + 2 * VROWS, mixed)


def attend_kernel(parities, begins, ends, core_ref, query_ref, *refs):
    x_count = query_ref.shape[0]
    keyval_refs = refs[: 2 * parities]
    video_bias_ref, audio_bias_ref, *rest = refs[2 * parities :]
    holds_keys = core_ref[0] == 0

    def rows_of(ref, first, last):
        rows = ref[:, :, :, first:last, :]
        if last - first == 8:
            rows = rows.astype(jnp.float32)
        return rows.reshape(-1, HD)

    video_pieces, audio_pieces = [], []
    for own, other in zip(keyval_refs[::2], keyval_refs[1::2]):
        for ref in (own, other):
            key = rows_of(ref, 0, VROWS)
            value = rows_of(ref, VROWS, 2 * VROWS)
            for first in range(0, key.shape[0], KEY_STEP):
                keys = slice(first, first + KEY_STEP)
                video_pieces.append((key[keys], value[keys]))
        own, other = (rows_of(ref, 2 * VROWS, BLOCK) for ref in (own, other))
        audio_pieces.append(
            (
                jnp.where(holds_keys, own, other).astype(jnp.bfloat16),
                jnp.where(holds_keys, other, own).astype(jnp.bfloat16),
            )
        )
    lane = lax.broadcasted_iota(jnp.int32, (1, 8, HD), 2)
    row = lax.broadcasted_iota(jnp.int32, (1, 8, HD), 1)
    in_row = lane // 16 == row
    field = lane % 16

    def attend(queries, pieces, bias_ref, state):
        first = 0
        for key, value in pieces:
            keys = slice(first, first + key.shape[0])
            first = keys.stop
            scores = lax.dot_general(
                queries, key, (((1,), (1,)), ((), ())), preferred_element_type=jnp.float32
            )
            scores = scores + bias_ref[0:1, keys]
            top = jnp.max(scores, axis=1, keepdims=True)
            top = top.astype(jnp.bfloat16).astype(jnp.float32)
            if state is not None:
                top = jnp.maximum(top, state[0])
            weights = jnp.exp2(scores - top)
            total = jnp.sum(weights, axis=1, keepdims=True)
            sums = jnp.dot(
                weights.astype(jnp.bfloat16), value, preferred_element_type=jnp.float32
            )
            if state is not None:
                keep = jnp.exp2(state[0] - top)
                total = total + state[1] * keep
                sums = sums + state[2] * keep
            state = top, total, sums
        return state

    def finish(top, total, sums):
        high = total.astype(jnp.bfloat16).astype(jnp.float32)
        groups = top.shape[0] // 8

        def wide(column):
            return jnp.broadcast_to(column, (column.shape[0], HD)).reshape(groups, 8, HD)

        stats = jnp.where(
            field == 0,
            wide(top),
            jnp.where(field == 1, wide(high), wide(total - high)),
        )
        stats = jnp.sum(jnp.where(in_row & (field < 3), stats, 0.0), axis=1)
        return (sums * pl.reciprocal(total)).astype(jnp.bfloat16), stats

    audio_rows = query_ref[:, :, 2 * VROWS :, :].astype(jnp.float32)
    audio_rows = audio_rows.reshape(x_count * NY // 2, 2, 8, HD)
    even, odd = audio_rows[:, 0], audio_rows[:, 1]
    low = low_rows(even.shape)
    audio_self = jnp.where(low, even, swap_halves(odd)).reshape(-1, HD).astype(jnp.bfloat16)
    audio_cross = jnp.where(low, swap_halves(even), odd).reshape(-1, HD).astype(jnp.bfloat16)
    video_self = query_ref[:, :, :VROWS, :].reshape(x_count * VTOK_DEV, HD)
    video_cross = query_ref[:, :, VROWS : 2 * VROWS, :].reshape(x_count * VTOK_DEV, HD)
    queries = (
        jnp.concatenate([video_self, audio_cross], axis=0),
        jnp.concatenate([video_cross, audio_self], axis=0),
    )
    pieces = (video_pieces, audio_pieces)
    biases = (video_bias_ref, audio_bias_ref)
    count = queries[0].shape[0]
    stats = []
    for kind in range(2):
        rows = slice(kind * count, (kind + 1) * count)
        state = attend(queries[kind], pieces[kind], biases[kind], None)
        top, total, sums = state
        if not ends:
            sums_ref, level_ref = rest
            sums_ref[rows, :] = (sums * pl.reciprocal(total)).astype(jnp.bfloat16)
            level_ref[rows, :] = jnp.broadcast_to(top + jnp.log2(total), (count, HD))
            continue
        if not begins:
            old_sums_ref, old_level_ref, _ = rest
            old_level = old_level_ref[rows, :]
            new_top = jnp.maximum(top, old_level.astype(jnp.bfloat16).astype(jnp.float32))
            keep, old_share = jnp.exp2(top - new_top), jnp.exp2(old_level - new_top)
            total = total * keep + old_share
            sums = sums * keep + old_sums_ref[rows, :].astype(jnp.float32) * old_share
            state = new_top, total, sums
        out_ref = rest[-1]
        rows, stat = finish(*state)
        stats.append(stat)
        start = kind * (VTOK_DEV + ATOK_DEV)
        for x in range(x_count):
            first = x * VTOK_DEV
            out_ref[x, start : start + VTOK_DEV, :] = rows[first : first + VTOK_DEV]
            first = x_count * VTOK_DEV + x * ATOK_DEV
            out_ref[x, start + VTOK_DEV : start + VTOK_DEV + ATOK_DEV, :] = rows[
                first : first + ATOK_DEV
            ]
    if not ends:
        return
    wide_stat, narrow_stat = VTOK_DEV // 8, ATOK_DEV // 8
    for x in range(x_count):
        picked = []
        for stat in stats:
            first = x * wide_stat
            picked.append(stat[first : first + wide_stat])
            first = x_count * wide_stat + x * narrow_stat
            picked.append(stat[first : first + narrow_stat])
        out_ref[x, OUT_ROWS:, :] = jnp.concatenate(picked, axis=0).astype(jnp.bfloat16)


def combine_kernel(part_ref, gate_ref, out_ref):
    parts = part_ref.shape[0]
    lane = lax.broadcasted_iota(jnp.int32, (1, 8, HD), 2)
    row = lax.broadcasted_iota(jnp.int32, (1, 8, HD), 1)
    in_row = lane // 16 == row
    source = lax.broadcasted_iota(jnp.int32, (HD, 2 * HD), 0) % 16
    target = lax.broadcasted_iota(jnp.int32, (HD, 2 * HD), 1) // HD
    source = jnp.where(source < 3, (source + 1) // 2, 2)
    pick = jnp.where(source == target, 1.0, 0.0).astype(jnp.bfloat16)
    tokens = VTOK_DEV + ATOK_DEV
    for head in range(HEADS_HERE):
        cols = slice(head * HD, (head + 1) * HD)
        tops, totals = [], []
        for part in range(parts):
            rows = part_ref[part, OUT_ROWS:, cols].astype(jnp.float32)
            rows = jnp.broadcast_to(rows[:, None, :], (STAT_ROWS, 8, HD))
            rows = jnp.where(in_row, rows, 0.0).reshape(OUT_ROWS, HD)
            fields = jnp.dot(
                rows.astype(jnp.bfloat16), pick, preferred_element_type=jnp.float32
            )
            tops.append(fields[:, :HD])
            totals.append(fields[:, HD:])
        top = tops[0]
        for other in tops[1:]:
            top = jnp.maximum(top, other)
        shares = [jnp.exp2(t - top) * total for t, total in zip(tops, totals)]
        inverse = 1.0 / sum(shares)
        merged = sum(
            part_ref[part, :OUT_ROWS, cols].astype(jnp.float32) * (shares[part] * inverse)
            for part in range(parts)
        )
        video = merged[:VTOK_DEV] + gate_ref[0:1, cols] * merged[tokens : tokens + VTOK_DEV]
        audio = merged[tokens + VTOK_DEV :] + gate_ref[1:2, cols] * merged[VTOK_DEV:tokens]
        out_ref[:, :VROWS, cols] = video.reshape(NY, VROWS, HD).astype(jnp.bfloat16)
        for pair in range(NY // 2):
            rows = audio[pair * 8 : pair * 8 + 8].astype(jnp.bfloat16)
            out_ref[2 * pair, VROWS:, cols] = rows
            out_ref[2 * pair + 1, VROWS:, cols] = rows


def place_kernel(place_ref, back_ref, video_ref, audio_ref):
    core = place_ref[0]
    odd = place_ref[1]
    half_groups = NY // 2
    for j in range(half_groups):
        group = core * half_groups + j
        cols = slice(j * GROUP, (j + 1) * GROUP)
        for s in range(2):
            video_ref[s * VROWS : (s + 1) * VROWS, cols] = back_ref[s, group, :VROWS, :]
        first, second = (back_ref[s, group, VROWS:, :].astype(jnp.float32) for s in range(2))
        low = low_rows(first.shape)
        audio_ref[:, cols] = jnp.where(
            odd == 0,
            jnp.where(low, first, swap_halves(second)),
            jnp.where(low, swap_halves(first), second),
        ).astype(jnp.bfloat16)


def whole(memory_space=pltpu.VMEM):
    return pl.BlockSpec(memory_space=memory_space)


def params():
    return pltpu.CompilerParams(vmem_limit_bytes=VMEM_LIMIT)


def shards(
    video_proj,
    audio_proj,
    video_gains,
    audio_gains,
    cross_gates,
    timestep,
    video_counts,
    audio_counts,
):
    core = lax.axis_index("tp")
    ring = ("yh", "aud")
    x_count = lax.axis_size("x")
    zq_count = lax.axis_size("zq")
    z_parity = lax.axis_index("zp")
    y_index = lax.axis_index(ring)
    packed = pl.pallas_call(
        pack_kernel,
        grid=(1,),
        out_shape=jax.ShapeDtypeStruct((PACK_ROWS, D // 2), jnp.bfloat16),
        in_specs=[
            whole(pltpu.SMEM),
            pl.BlockSpec(video_proj.shape, lambda i: (0, 0, 0)),
            pl.BlockSpec(audio_proj.shape, lambda i: (0, 0, 0)),
            pl.BlockSpec(video_gains.shape, lambda i: (0, 0)),
            pl.BlockSpec(audio_gains.shape, lambda i: (0, 0)),
        ],
        out_specs=pl.BlockSpec((PACK_ROWS, D // 2), lambda i: (0, 0)),
        compiler_params=pltpu.CompilerParams(vmem_limit_bytes=PACK_VMEM),
        name="pack",
    )(core[None], video_proj, audio_proj, video_gains, audio_gains)
    packed = lax.all_gather(packed, "tp", axis=0)
    blocks = pl.pallas_call(
        norm_kernel,
        out_shape=jax.ShapeDtypeStruct((NY, 2 * BLOCK, GROUP), jnp.bfloat16),
        in_specs=[whole(pltpu.SMEM)] + [whole()] * 5,
        out_specs=whole(),
        compiler_params=params(),
        name="norm",
    )(core[None], video_proj, audio_proj, video_gains, audio_gains, packed)

    x_index = lax.axis_index("x")
    aud_first = np.arange(NY // YH)
    parities = jnp.stack([z_parity, 1 - z_parity])
    halves = jnp.stack([core, 1 - core])

    def allowed(counts):
        here = counts.reshape(YH, x_count, zq_count, ZP)
        here = lax.dynamic_index_in_dim(here, x_index, 1, keepdims=False)
        here = here.transpose(2, 1, 0)
        return jnp.where(z_parity == 0, here, here[::-1])

    def bias(live):
        return jnp.where(live, 0.0, MASKED).astype(jnp.float32).reshape(1, -1)

    video_first = (
        aud_first[None, :, None] * (2 * VROWS)
        + halves[:, None, None] * VROWS
        + np.arange(VROWS)[None, None, :]
    )
    audio_first = aud_first[:, None] * 8 + np.arange(8)[None, :]
    allowed_video, allowed_audio = allowed(video_counts), allowed(audio_counts)
    biases = [
        (
            bias(video_first[:, None, None] < allowed_video[parity][None, :, :, None, None]),
            bias(audio_first < allowed_audio[parity][..., None, None]),
        )
        for parity in range(ZP)
    ]
    places = jnp.stack([core, y_index % 2])
    gates = lax.dynamic_index_in_dim(cross_gates, timestep[0], 1, keepdims=False)
    gates, packed = lax.optimization_barrier((gates, packed))
    gates = lax.all_gather(gates, "tp", axis=0)
    gates = lax.dynamic_slice(
        gates,
        (y_index // (NY // 2), 0, (y_index % (NY // 2)) * GROUP),
        (1, 2, GROUP),
    )[0].astype(jnp.float32)
    blocks = lax.all_to_all(blocks, ring, split_axis=0, concat_axis=0)
    keyval, queries = blocks[:, :BLOCK], blocks[:, BLOCK:]
    biases = [jnp.concatenate(part, axis=1) for part in zip(*biases)]
    keyval, queries, gates, biases, places = lax.optimization_barrier(
        (keyval, queries, gates, biases, places)
    )
    keyval = lax.all_gather(keyval, "zq", axis=0, tiled=True)
    keyval, queries = lax.optimization_barrier((keyval, queries))
    queries = lax.all_gather(queries, "x", axis=0)
    full_shape = (zq_count, YH, NY // YH, BLOCK, GROUP)

    ways = [
        (z * 2 + c, (z + 1 - 2 * c) % (ZP * zq_count) * 2 + c)
        for z in range(ZP * zq_count)
        for c in range(2)
    ]
    swap = [(0, 1), (1, 0)]
    far = lax.ppermute(keyval, ("zq", "zp", "tp"), ways)
    keyval_other = lax.ppermute(keyval, "tp", swap)
    far, queries = lax.optimization_barrier((far, queries))
    far_other = lax.ppermute(far, "tp", swap)
    near = [keyval.reshape(full_shape), keyval_other.reshape(full_shape)]
    far = [far.reshape(full_shape), far_other.reshape(full_shape)]

    def attend(keyvals, video_bias, audio_bias, state, ends):
        parities = len(keyvals) // 2
        rows = 2 * x_count * (VTOK_DEV + ATOK_DEV)
        state_spec = pl.BlockSpec((rows, HD), lambda h: (0, h))
        if ends:
            out_shape = jax.ShapeDtypeStruct(
                (x_count, OUT_ROWS + STAT_ROWS, GROUP), jnp.bfloat16
            )
            out_specs = pl.BlockSpec(
                (x_count, OUT_ROWS + STAT_ROWS, HD), lambda h: (0, 0, h)
            )
        else:
            out_shape = tuple(
                jax.ShapeDtypeStruct((rows, GROUP), dtype)
                for dtype in (jnp.bfloat16, jnp.float32)
            )
            out_specs = (state_spec,) * 2
        keyval_spec = pl.BlockSpec(full_shape[:-1] + (HD,), lambda h: (0, 0, 0, 0, h))
        return pl.pallas_call(
            functools.partial(attend_kernel, parities, not state, ends),
            grid=(HEADS_HERE,),
            out_shape=out_shape,
            in_specs=[
                whole(pltpu.SMEM),
                pl.BlockSpec((x_count, NY, BLOCK, HD), lambda h: (0, 0, 0, h)),
                *[keyval_spec] * len(keyvals),
                pl.BlockSpec(video_bias.shape, lambda h: (0, 0)),
                pl.BlockSpec(audio_bias.shape, lambda h: (0, 0)),
                *[state_spec] * len(state),
            ],
            out_specs=out_specs,
            compiler_params=params(),
            name="attend_near" if not ends else "attend",
        )(core[None], queries, *keyvals, video_bias, audio_bias, *state)

    partial = attend(near + far, *biases, (), True)
    partial = lax.all_to_all(partial, "x", split_axis=0, concat_axis=0)
    back = pl.pallas_call(
        combine_kernel,
        out_shape=jax.ShapeDtypeStruct((NY, BACK_ROWS, GROUP), jnp.bfloat16),
        in_specs=[whole(), whole()],
        out_specs=whole(),
        compiler_params=params(),
        name="combine",
    )(partial, gates)
    back = lax.all_to_all(back, ring, split_axis=0, concat_axis=0)
    back = lax.all_gather(back, "tp", axis=0)
    return pl.pallas_call(
        place_kernel,
        out_shape=(
            jax.ShapeDtypeStruct((2 * VROWS, D // 2), jnp.bfloat16),
            jax.ShapeDtypeStruct((2 * AROWS, D // 2), jnp.bfloat16),
        ),
        in_specs=[whole(pltpu.SMEM), whole()],
        out_specs=(whole(), whole()),
        compiler_params=params(),
        name="place",
    )(places, back)


def solution(mesh):
    vid = mesh.devices.shape[0]
    cut = (YH, vid // (YH * ZQ * ZP), ZQ, ZP)
    axes = ("yh", "x", "zq", "zp", "aud", "tp")
    fine = Mesh(mesh.devices.reshape(cut + mesh.devices.shape[1:]), axes)
    tokens = axes[:-1]
    in_specs = (
        P(None, tokens, "tp"),
        P(None, tokens, "tp"),
        P(None, "tp"),
        P(None, "tp"),
        P(None, None, "tp"),
        P(),
        P(),
        P(),
    )
    out_specs = (P(tokens, "tp"), P(tokens, "tp"))
    return jax.shard_map(
        shards, mesh=fine, in_specs=in_specs, out_specs=out_specs, check_vma=False
    )
```

```python
import math

import jax
import jax.numpy as jnp
import numpy as np
from jax import lax
from jax.experimental import pallas as pl
from jax.experimental.pallas import tpu as pltpu
from jax.sharding import Mesh
from jax.sharding import PartitionSpec as P

D = 3072
HD = 128
VTOK_DEV = 128
ATOK_DEV = 32
EPSILON = 1e-06
MASKED = -1e30

YH = 2
NY = 8
ZP = 2
ZQ = 4
GROUP = D // NY
HEADS_HERE = GROUP // HD
VROWS = 16
AROWS = 4
BLOCK = 2 * VROWS + 2 * AROWS
OUT_ROWS = 2 * (VTOK_DEV + ATOK_DEV)
STAT_FIELDS = 4
STATS_PER_ROW = HD // STAT_FIELDS
STAT_USED = OUT_ROWS // STATS_PER_ROW
STAT_ROWS = 16
BACK_ROWS = VROWS + 8
AUDIO_ROW = 4 * VROWS
SMALL_ROW = AUDIO_ROW + 4 * 2 * AROWS
PACK_ROWS = SMALL_ROW + 32
KEY_STEP = 256
SCORE_SCALE = HD ** (-0.5) * math.log2(math.e)
VMEM_LIMIT = 48 * 1024 * 1024
PACK_VMEM = 60 * 1024 * 1024


def low_rows(shape):
    return lax.broadcasted_iota(jnp.int32, shape, len(shape) - 2) % 8 < 4


def swap_halves(rows):
    return pltpu.roll(rows, 4, axis=rows.ndim - 2)


def pack_kernel(core_ref, video_ref, audio_ref, video_gains_ref, audio_gains_ref, out_ref):
    first = pl.multiple_of((1 - core_ref[0]) * VROWS, VROWS)
    for array in range(4):
        row = array * VROWS
        out_ref[row : row + VROWS, :] = video_ref[array, pl.ds(first, VROWS), :]
        row = AUDIO_ROW + array * 8
        out_ref[row : row + 8, :] = audio_ref[array]
    gains = [video_gains_ref[...], audio_gains_ref[...]]
    rest = jnp.concatenate(gains + [jnp.zeros_like(gains[0][:2])], axis=0)
    pieces = []
    for _ in range(3):
        piece = rest.astype(jnp.bfloat16).astype(jnp.float32)
        pieces.append(piece)
        rest = rest - piece
    pieces.append(jnp.zeros_like(rest))
    out_ref[SMALL_ROW:, :] = jnp.concatenate(pieces, axis=0).astype(jnp.bfloat16)


def norm_kernel(
    core_ref,
    video_ref,
    audio_ref,
    video_gains_ref,
    audio_gains_ref,
    packed_ref,
    out_ref,
):
    core = core_ref[0]
    at_zero = core == 0
    own_first = pl.multiple_of(core * VROWS, VROWS)
    small = packed_ref[1 - core, SMALL_ROW:, :].astype(jnp.float32)
    other_gains = small[0:8] + small[8:16] + small[16:24]
    own_gains = jnp.concatenate([video_gains_ref[...], audio_gains_ref[...]], axis=0)

    def ordered(own, other):
        return [jnp.where(at_zero, own, other), jnp.where(at_zero, other, own)]

    gains = ordered(own_gains, other_gains[:6])
    half_groups = NY // 2

    def normed(halves, gain_row, extra):
        total = sum(jnp.sum(v * v, axis=1, keepdims=True) for v in halves)
        inverse = lax.rsqrt(total / D + EPSILON)
        return [
            v * inverse * (gains[s][gain_row : gain_row + 1, :] * extra)
            for s, v in enumerate(halves)
        ]

    def spread(row, halves):
        count = halves[0].shape[0]
        for group in range(NY):
            col = (group % half_groups) * GROUP
            out_ref[group, row : row + count, :] = halves[group // half_groups][
                :, col : col + GROUP
            ].astype(jnp.bfloat16)

    def video(array):
        first = array * VROWS
        return ordered(
            video_ref[array, pl.ds(own_first, VROWS), :].astype(jnp.float32),
            packed_ref[1 - core, first : first + VROWS, :].astype(jnp.float32),
        )

    def audio(array):
        first = AUDIO_ROW + array * 8
        return ordered(
            audio_ref[array].astype(jnp.float32),
            packed_ref[1 - core, first : first + 8, :].astype(jnp.float32),
        )

    spread(0, normed(video(2), 2, 1.0))
    spread(VROWS, video(3))
    audio_key = normed(audio(2), 5, 1.0)
    audio_value = audio(3)
    spread(
        2 * VROWS,
        [jnp.where(at_zero, k, v) for k, v in zip(audio_key, audio_value)],
    )
    spread(BLOCK, normed(video(0), 0, SCORE_SCALE))
    spread(BLOCK + VROWS, normed(video(1), 1, SCORE_SCALE))
    audio_self = normed(audio(0), 3, SCORE_SCALE)
    audio_cross = normed(audio(1), 4, SCORE_SCALE)
    mixed = []
    for own, other in zip(audio_self, audio_cross):
        low = low_rows(own.shape)
        mixed.append(
            jnp.where(
                at_zero,
                jnp.where(low, own, swap_halves(other)),
                jnp.where(low, swap_halves(own), other),
            )
        )
    spread(BLOCK + 2 * VROWS, mixed)


def stat_places():
    shape = (1, STATS_PER_ROW // 8, 8, HD)
    tile, row, lane = (lax.broadcasted_iota(jnp.int32, shape, i) for i in (1, 2, 3))
    return lane // STAT_FIELDS == tile * 8 + row, lane % STAT_FIELDS


def attend_kernel(core_ref, query_ref, *refs):
    x_count = query_ref.shape[0]
    *keyval_refs, video_bias_ref, audio_bias_ref, out_ref = refs
    holds_keys = core_ref[0] == 0

    def rows_of(ref, first, last):
        rows = ref[:, :, :, first:last, :]
        if last - first == 8:
            rows = rows.astype(jnp.float32)
        return rows.reshape(-1, HD)

    video_pieces, audio_pieces = [], []
    for own, other in zip(keyval_refs[::2], keyval_refs[1::2]):
        for ref in (own, other):
            key = rows_of(ref, 0, VROWS)
            value = rows_of(ref, VROWS, 2 * VROWS)
            for first in range(0, key.shape[0], KEY_STEP):
                keys = slice(first, first + KEY_STEP)
                video_pieces.append((key[keys], value[keys]))
        own, other = (rows_of(ref, 2 * VROWS, BLOCK) for ref in (own, other))
        audio_pieces.append(
            (
                jnp.where(holds_keys, own, other).astype(jnp.bfloat16),
                jnp.where(holds_keys, other, own).astype(jnp.bfloat16),
            )
        )
    in_place, field = stat_places()

    def attend(queries, pieces, bias_ref):
        state, first = None, 0
        for key, value in pieces:
            keys = slice(first, first + key.shape[0])
            first = keys.stop
            scores = lax.dot_general(
                queries, key, (((1,), (1,)), ((), ())), preferred_element_type=jnp.float32
            )
            scores = scores + bias_ref[0:1, keys]
            top = jnp.max(scores, axis=1, keepdims=True)
            top = top.astype(jnp.bfloat16).astype(jnp.float32)
            if state is not None:
                top = jnp.maximum(top, state[0])
            weights = jnp.exp2(scores - top)
            total = sum(weights[:, i : i + HD] for i in range(0, weights.shape[1], HD))
            sums = jnp.dot(
                weights.astype(jnp.bfloat16), value, preferred_element_type=jnp.float32
            )
            if state is not None:
                keep = jnp.exp2(state[0] - top)
                total = total + state[1] * keep
                sums = sums + state[2] * keep
            state = top, total, sums
        top, total, sums = state
        return top, jnp.sum(total, axis=1, keepdims=True), sums

    def finish(top, total, sums):
        high = total.astype(jnp.bfloat16).astype(jnp.float32)

        def wide(column):
            wide_column = jnp.broadcast_to(column, (column.shape[0], HD))
            return wide_column.reshape(-1, STATS_PER_ROW // 8, 8, HD)

        stats = jnp.where(
            field == 0,
            wide(top),
            jnp.where(field == 1, wide(high), wide(total - high)),
        )
        stats = jnp.sum(jnp.where(in_place & (field < 3), stats, 0.0), axis=(1, 2))
        return (sums * (1.0 / total)).astype(jnp.bfloat16), stats

    audio_rows = query_ref[:, :, 2 * VROWS :, :].astype(jnp.float32)
    audio_rows = audio_rows.reshape(x_count * NY // 2, 2, 8, HD)
    even, odd = audio_rows[:, 0], audio_rows[:, 1]
    low = low_rows(even.shape)
    audio_self = jnp.where(low, even, swap_halves(odd)).reshape(-1, HD).astype(jnp.bfloat16)
    audio_cross = jnp.where(low, swap_halves(even), odd).reshape(-1, HD).astype(jnp.bfloat16)
    video_self = query_ref[:, :, :VROWS, :].reshape(x_count * VTOK_DEV, HD)
    video_cross = query_ref[:, :, VROWS : 2 * VROWS, :].reshape(x_count * VTOK_DEV, HD)
    queries = (
        jnp.concatenate([video_self, audio_cross], axis=0),
        jnp.concatenate([video_cross, audio_self], axis=0),
    )
    pieces = (video_pieces, audio_pieces)
    biases = (video_bias_ref, audio_bias_ref)
    stats = []
    for kind in range(2):
        rows, stat = finish(*attend(queries[kind], pieces[kind], biases[kind]))
        stats.append(stat)
        start = kind * (VTOK_DEV + ATOK_DEV)
        for x in range(x_count):
            first = x * VTOK_DEV
            out_ref[x, start : start + VTOK_DEV, :] = rows[first : first + VTOK_DEV]
            first = x_count * VTOK_DEV + x * ATOK_DEV
            out_ref[x, start + VTOK_DEV : start + VTOK_DEV + ATOK_DEV, :] = rows[
                first : first + ATOK_DEV
            ]
    wide_stat, narrow_stat = VTOK_DEV // STATS_PER_ROW, ATOK_DEV // STATS_PER_ROW
    for x in range(x_count):
        picked = []
        for stat in stats:
            first = x * wide_stat
            picked.append(stat[first : first + wide_stat])
            first = x_count * wide_stat + x * narrow_stat
            picked.append(stat[first : first + narrow_stat])
        picked.append(jnp.zeros((STAT_ROWS - STAT_USED, HD), jnp.float32))
        out_ref[x, OUT_ROWS:, :] = jnp.concatenate(picked, axis=0).astype(jnp.bfloat16)


def combine_kernel(part_ref, gate_ref, out_ref):
    parts = part_ref.shape[0]
    in_place, _ = stat_places()
    source = lax.broadcasted_iota(jnp.int32, (HD, 2 * HD), 0) % STAT_FIELDS
    target = lax.broadcasted_iota(jnp.int32, (HD, 2 * HD), 1) // HD
    source = jnp.where(source < 3, (source + 1) // 2, 2)
    pick = jnp.where(source == target, 1.0, 0.0).astype(jnp.bfloat16)
    tokens = VTOK_DEV + ATOK_DEV
    for head in range(HEADS_HERE):
        cols = slice(head * HD, (head + 1) * HD)
        tops, totals = [], []
        for part in range(parts):
            rows = part_ref[part, OUT_ROWS:, cols].astype(jnp.float32)[:STAT_USED]
            rows = jnp.broadcast_to(
                rows[:, None, None, :], (STAT_USED, STATS_PER_ROW // 8, 8, HD)
            )
            rows = jnp.where(in_place, rows, 0.0).reshape(OUT_ROWS, HD)
            fields = jnp.dot(
                rows.astype(jnp.bfloat16), pick, preferred_element_type=jnp.float32
            )
            tops.append(fields[:, :HD])
            totals.append(fields[:, HD:])
        top = tops[0]
        for other in tops[1:]:
            top = jnp.maximum(top, other)
        shares = [jnp.exp2(t - top) * total for t, total in zip(tops, totals)]
        inverse = 1.0 / sum(shares)
        merged = sum(
            part_ref[part, :OUT_ROWS, cols].astype(jnp.float32) * (shares[part] * inverse)
            for part in range(parts)
        )
        video = merged[:VTOK_DEV] + gate_ref[0:1, cols] * merged[tokens : tokens + VTOK_DEV]
        audio = merged[tokens + VTOK_DEV :] + gate_ref[1:2, cols] * merged[VTOK_DEV:tokens]
        out_ref[:, :VROWS, cols] = video.reshape(NY, VROWS, HD).astype(jnp.bfloat16)
        for pair in range(NY // 2):
            rows = audio[pair * 8 : pair * 8 + 8].astype(jnp.bfloat16)
            out_ref[2 * pair, VROWS:, cols] = rows
            out_ref[2 * pair + 1, VROWS:, cols] = rows


def place_kernel(place_ref, back_ref, video_ref, audio_ref):
    core = place_ref[0]
    odd = place_ref[1]
    half_groups = NY // 2
    for j in range(half_groups):
        group = core * half_groups + j
        cols = slice(j * GROUP, (j + 1) * GROUP)
        for s in range(2):
            video_ref[s * VROWS : (s + 1) * VROWS, cols] = back_ref[s, group, :VROWS, :]
        first, second = (back_ref[s, group, VROWS:, :].astype(jnp.float32) for s in range(2))
        low = low_rows(first.shape)
        audio_ref[:, cols] = jnp.where(
            odd == 0,
            jnp.where(low, first, swap_halves(second)),
            jnp.where(low, swap_halves(first), second),
        ).astype(jnp.bfloat16)


def whole(memory_space=pltpu.VMEM):
    return pl.BlockSpec(memory_space=memory_space)


def params():
    return pltpu.CompilerParams(vmem_limit_bytes=VMEM_LIMIT)


def shards(
    video_proj,
    audio_proj,
    video_gains,
    audio_gains,
    cross_gates,
    timestep,
    video_counts,
    audio_counts,
):
    core = lax.axis_index("tp")
    ring = ("yh", "aud")
    x_count = lax.axis_size("x")
    zq_count = lax.axis_size("zq")
    z_parity = lax.axis_index("zp")
    y_index = lax.axis_index(ring)
    packed = pl.pallas_call(
        pack_kernel,
        grid=(1,),
        out_shape=jax.ShapeDtypeStruct((PACK_ROWS, D // 2), jnp.bfloat16),
        in_specs=[
            whole(pltpu.SMEM),
            pl.BlockSpec(video_proj.shape, lambda i: (0, 0, 0)),
            pl.BlockSpec(audio_proj.shape, lambda i: (0, 0, 0)),
            pl.BlockSpec(video_gains.shape, lambda i: (0, 0)),
            pl.BlockSpec(audio_gains.shape, lambda i: (0, 0)),
        ],
        out_specs=pl.BlockSpec((PACK_ROWS, D // 2), lambda i: (0, 0)),
        compiler_params=pltpu.CompilerParams(vmem_limit_bytes=PACK_VMEM),
        name="pack",
    )(core[None], video_proj, audio_proj, video_gains, audio_gains)
    packed = lax.all_gather(packed, "tp", axis=0)
    blocks = pl.pallas_call(
        norm_kernel,
        out_shape=jax.ShapeDtypeStruct((NY, 2 * BLOCK, GROUP), jnp.bfloat16),
        in_specs=[whole(pltpu.SMEM)] + [whole()] * 5,
        out_specs=whole(),
        compiler_params=params(),
        name="norm",
    )(core[None], video_proj, audio_proj, video_gains, audio_gains, packed)

    x_index = lax.axis_index("x")
    aud_first = np.arange(NY // YH)
    parities = jnp.stack([z_parity, 1 - z_parity])
    halves = jnp.stack([core, 1 - core])

    def allowed(counts):
        here = counts.reshape(YH, x_count, zq_count, ZP)
        here = lax.dynamic_index_in_dim(here, x_index, 1, keepdims=False)
        here = here.transpose(2, 1, 0)
        return jnp.where(z_parity == 0, here, here[::-1])

    def bias(live):
        return jnp.where(live, 0.0, MASKED).astype(jnp.float32).reshape(1, -1)

    video_first = (
        aud_first[None, :, None] * (2 * VROWS)
        + halves[:, None, None] * VROWS
        + np.arange(VROWS)[None, None, :]
    )
    audio_first = aud_first[:, None] * 8 + np.arange(8)[None, :]
    allowed_video, allowed_audio = allowed(video_counts), allowed(audio_counts)
    biases = [
        (
            bias(video_first[:, None, None] < allowed_video[parity][None, :, :, None, None]),
            bias(audio_first < allowed_audio[parity][..., None, None]),
        )
        for parity in range(ZP)
    ]
    places = jnp.stack([core, y_index % 2])
    gates = lax.dynamic_index_in_dim(cross_gates, timestep[0], 1, keepdims=False)
    gates, packed = lax.optimization_barrier((gates, packed))
    gates = lax.all_gather(gates, "tp", axis=0)
    gates = lax.dynamic_slice(
        gates,
        (y_index // (NY // 2), 0, (y_index % (NY // 2)) * GROUP),
        (1, 2, GROUP),
    )[0].astype(jnp.float32)
    blocks = lax.all_to_all(blocks, ring, split_axis=0, concat_axis=0)
    keyval, queries = blocks[:, :BLOCK], blocks[:, BLOCK:]
    biases = [jnp.concatenate(part, axis=1) for part in zip(*biases)]
    keyval, queries, gates, biases, places = lax.optimization_barrier(
        (keyval, queries, gates, biases, places)
    )
    keyval = lax.all_gather(keyval, "zq", axis=0, tiled=True)
    keyval, queries = lax.optimization_barrier((keyval, queries))
    queries = lax.all_gather(queries, "x", axis=0)
    full_shape = (zq_count, YH, NY // YH, BLOCK, GROUP)

    ways = [
        (z * 2 + c, (z + 1 - 2 * c) % (ZP * zq_count) * 2 + c)
        for z in range(ZP * zq_count)
        for c in range(2)
    ]
    swap = [(0, 1), (1, 0)]
    far = lax.ppermute(keyval, ("zq", "zp", "tp"), ways)
    keyval_other = lax.ppermute(keyval, "tp", swap)
    far, queries = lax.optimization_barrier((far, queries))
    far_other = lax.ppermute(far, "tp", swap)
    near = [keyval.reshape(full_shape), keyval_other.reshape(full_shape)]
    far = [far.reshape(full_shape), far_other.reshape(full_shape)]

    keyval_spec = pl.BlockSpec(full_shape[:-1] + (HD,), lambda h: (0, 0, 0, 0, h))
    partial = pl.pallas_call(
        attend_kernel,
        grid=(HEADS_HERE,),
        out_shape=jax.ShapeDtypeStruct(
            (x_count, OUT_ROWS + STAT_ROWS, GROUP), jnp.bfloat16
        ),
        in_specs=[
            whole(pltpu.SMEM),
            pl.BlockSpec((x_count, NY, BLOCK, HD), lambda h: (0, 0, 0, h)),
            *[keyval_spec] * 4,
            *[pl.BlockSpec(bias.shape, lambda h: (0, 0)) for bias in biases],
        ],
        out_specs=pl.BlockSpec((x_count, OUT_ROWS + STAT_ROWS, HD), lambda h: (0, 0, h)),
        compiler_params=params(),
        name="attend",
    )(core[None], queries, *near, *far, *biases)
    partial = lax.all_to_all(partial, "x", split_axis=0, concat_axis=0)
    back = pl.pallas_call(
        combine_kernel,
        out_shape=jax.ShapeDtypeStruct((NY, BACK_ROWS, GROUP), jnp.bfloat16),
        in_specs=[whole(), whole()],
        out_specs=whole(),
        compiler_params=params(),
        name="combine",
    )(partial, gates)
    back = lax.all_to_all(back, ring, split_axis=0, concat_axis=0)
    back = lax.all_gather(back, "tp", axis=0)
    return pl.pallas_call(
        place_kernel,
        out_shape=(
            jax.ShapeDtypeStruct((2 * VROWS, D // 2), jnp.bfloat16),
            jax.ShapeDtypeStruct((2 * AROWS, D // 2), jnp.bfloat16),
        ),
        in_specs=[whole(pltpu.SMEM), whole()],
        out_specs=(whole(), whole()),
        compiler_params=params(),
        name="place",
    )(places, back)


def solution(mesh):
    vid = mesh.devices.shape[0]
    cut = (YH, vid // (YH * ZQ * ZP), ZQ, ZP)
    axes = ("yh", "x", "zq", "zp", "aud", "tp")
    fine = Mesh(mesh.devices.reshape(cut + mesh.devices.shape[1:]), axes)
    tokens = axes[:-1]
    in_specs = (
        P(None, tokens, "tp"),
        P(None, tokens, "tp"),
        P(None, "tp"),
        P(None, "tp"),
        P(None, None, "tp"),
        P(),
        P(),
        P(),
    )
    out_specs = (P(tokens, "tp"), P(tokens, "tp"))
    return jax.shard_map(
        shards, mesh=fine, in_specs=in_specs, out_specs=out_specs, check_vma=False
    )
```

```python
import math

import jax
import jax.numpy as jnp
import numpy as np
from jax import lax
from jax.experimental import pallas as pl
from jax.experimental.pallas import tpu as pltpu
from jax.sharding import Mesh
from jax.sharding import PartitionSpec as P

D = 3072
HD = 128
VTOK_DEV = 128
ATOK_DEV = 32
EPSILON = 1e-06
MASKED = -1e30

YH = 2
AH = 2
AL = 2
RING = 8
GROUP = D // RING
HEADS_HERE = GROUP // HD
VROWS = 16
AROWS = 4
BLOCK = 2 * VROWS + 2 * AROWS
OUT_ROWS = 2 * (VTOK_DEV + ATOK_DEV)
STAT_FIELDS = 4
STATS_PER_ROW = HD // STAT_FIELDS
STAT_USED = OUT_ROWS // STATS_PER_ROW
STAT_ROWS = 16
BACK_ROWS = VROWS + 8
AUDIO_ROW = 4 * VROWS
SMALL_ROW = AUDIO_ROW + 4 * 2 * AROWS
PACK_ROWS = SMALL_ROW + 32
KEY_STEP = 256
SCORE_SCALE = HD ** (-0.5) * math.log2(math.e)
VMEM_LIMIT = 48 * 1024 * 1024
PACK_VMEM = 60 * 1024 * 1024


def low_rows(shape):
    return lax.broadcasted_iota(jnp.int32, shape, len(shape) - 2) % 8 < 4


def swap_halves(rows):
    return pltpu.roll(rows, 4, axis=rows.ndim - 2)


def pack_kernel(core_ref, video_ref, audio_ref, video_gains_ref, audio_gains_ref, out_ref):
    first = pl.multiple_of((1 - core_ref[0]) * VROWS, VROWS)
    for array in range(4):
        row = array * VROWS
        out_ref[row : row + VROWS, :] = video_ref[array, pl.ds(first, VROWS), :]
        row = AUDIO_ROW + array * 8
        out_ref[row : row + 8, :] = audio_ref[array]
    gains = [video_gains_ref[...], audio_gains_ref[...]]
    rest = jnp.concatenate(gains + [jnp.zeros_like(gains[0][:2])], axis=0)
    pieces = []
    for _ in range(3):
        piece = rest.astype(jnp.bfloat16).astype(jnp.float32)
        pieces.append(piece)
        rest = rest - piece
    pieces.append(jnp.zeros_like(rest))
    out_ref[SMALL_ROW:, :] = jnp.concatenate(pieces, axis=0).astype(jnp.bfloat16)


def norm_kernel(
    core_ref,
    video_ref,
    audio_ref,
    video_gains_ref,
    audio_gains_ref,
    packed_ref,
    out_ref,
):
    core = core_ref[0]
    at_zero = core == 0
    own_first = pl.multiple_of(core * VROWS, VROWS)
    small = packed_ref[1 - core, SMALL_ROW:, :].astype(jnp.float32)
    other_gains = small[0:8] + small[8:16] + small[16:24]
    own_gains = jnp.concatenate([video_gains_ref[...], audio_gains_ref[...]], axis=0)

    def ordered(own, other):
        return [jnp.where(at_zero, own, other), jnp.where(at_zero, other, own)]

    gains = ordered(own_gains, other_gains[:6])
    half_groups = RING // 2

    def normed(halves, gain_row, extra):
        total = sum(jnp.sum(v * v, axis=1, keepdims=True) for v in halves)
        inverse = lax.rsqrt(total / D + EPSILON)
        return [
            v * inverse * (gains[s][gain_row : gain_row + 1, :] * extra)
            for s, v in enumerate(halves)
        ]

    def spread(row, halves):
        count = halves[0].shape[0]
        for group in range(RING):
            col = (group % half_groups) * GROUP
            out_ref[group, row : row + count, :] = halves[group // half_groups][
                :, col : col + GROUP
            ].astype(jnp.bfloat16)

    def video(array):
        first = array * VROWS
        return ordered(
            video_ref[array, pl.ds(own_first, VROWS), :].astype(jnp.float32),
            packed_ref[1 - core, first : first + VROWS, :].astype(jnp.float32),
        )

    def audio(array):
        first = AUDIO_ROW + array * 8
        return ordered(
            audio_ref[array].astype(jnp.float32),
            packed_ref[1 - core, first : first + 8, :].astype(jnp.float32),
        )

    spread(0, normed(video(2), 2, 1.0))
    spread(VROWS, video(3))
    audio_key = normed(audio(2), 5, 1.0)
    audio_value = audio(3)
    spread(
        2 * VROWS,
        [jnp.where(at_zero, k, v) for k, v in zip(audio_key, audio_value)],
    )
    spread(BLOCK, normed(video(0), 0, SCORE_SCALE))
    spread(BLOCK + VROWS, normed(video(1), 1, SCORE_SCALE))
    audio_self = normed(audio(0), 3, SCORE_SCALE)
    audio_cross = normed(audio(1), 4, SCORE_SCALE)
    mixed = []
    for own, other in zip(audio_self, audio_cross):
        low = low_rows(own.shape)
        mixed.append(
            jnp.where(
                at_zero,
                jnp.where(low, own, swap_halves(other)),
                jnp.where(low, swap_halves(own), other),
            )
        )
    spread(BLOCK + 2 * VROWS, mixed)


def stat_places():
    shape = (1, STATS_PER_ROW // 8, 8, HD)
    tile, row, lane = (lax.broadcasted_iota(jnp.int32, shape, i) for i in (1, 2, 3))
    return lane // STAT_FIELDS == tile * 8 + row, lane % STAT_FIELDS


def attend_kernel(core_ref, query_ref, *refs):
    x_count = query_ref.shape[0]
    *keyval_refs, video_bias_ref, audio_bias_ref, out_ref = refs
    holds_keys = core_ref[0] == 0

    def rows_of(ref, first, last):
        rows = ref[:, :, :, first:last, :]
        if last - first == 8:
            rows = rows.astype(jnp.float32)
        return rows.reshape(-1, HD)

    video_pieces, audio_pieces = [], []
    for own, other in zip(keyval_refs[::2], keyval_refs[1::2]):
        for ref in (own, other):
            key = rows_of(ref, 0, VROWS)
            value = rows_of(ref, VROWS, 2 * VROWS)
            for first in range(0, key.shape[0], KEY_STEP):
                keys = slice(first, first + KEY_STEP)
                video_pieces.append((key[keys], value[keys]))
        own, other = (rows_of(ref, 2 * VROWS, BLOCK) for ref in (own, other))
        audio_pieces.append(
            (
                jnp.where(holds_keys, own, other).astype(jnp.bfloat16),
                jnp.where(holds_keys, other, own).astype(jnp.bfloat16),
            )
        )
    in_place, field = stat_places()

    def attend(queries, pieces, bias_ref):
        state, first = None, 0
        for key, value in pieces:
            keys = slice(first, first + key.shape[0])
            first = keys.stop
            scores = lax.dot_general(
                queries, key, (((1,), (1,)), ((), ())), preferred_element_type=jnp.float32
            )
            scores = scores + bias_ref[0:1, keys]
            top = jnp.max(scores, axis=1, keepdims=True)
            top = top.astype(jnp.bfloat16).astype(jnp.float32)
            if state is not None:
                top = jnp.maximum(top, state[0])
            weights = jnp.exp2(scores - top)
            total = sum(weights[:, i : i + HD] for i in range(0, weights.shape[1], HD))
            sums = jnp.dot(
                weights.astype(jnp.bfloat16), value, preferred_element_type=jnp.float32
            )
            if state is not None:
                keep = jnp.exp2(state[0] - top)
                total = total + state[1] * keep
                sums = sums + state[2] * keep
            state = top, total, sums
        top, total, sums = state
        return top, jnp.sum(total, axis=1, keepdims=True), sums

    def finish(top, total, sums):
        high = total.astype(jnp.bfloat16).astype(jnp.float32)

        def wide(column):
            wide_column = jnp.broadcast_to(column, (column.shape[0], HD))
            return wide_column.reshape(-1, STATS_PER_ROW // 8, 8, HD)

        stats = jnp.where(
            field == 0,
            wide(top),
            jnp.where(field == 1, wide(high), wide(total - high)),
        )
        stats = jnp.sum(jnp.where(in_place & (field < 3), stats, 0.0), axis=(1, 2))
        return (sums * (1.0 / total)).astype(jnp.bfloat16), stats

    audio_rows = query_ref[:, :, 2 * VROWS :, :].astype(jnp.float32)
    audio_rows = audio_rows.reshape(x_count * RING // 2, 2, 8, HD)
    even, odd = audio_rows[:, 0], audio_rows[:, 1]
    low = low_rows(even.shape)
    audio_self = jnp.where(low, even, swap_halves(odd)).reshape(-1, HD).astype(jnp.bfloat16)
    audio_cross = jnp.where(low, swap_halves(even), odd).reshape(-1, HD).astype(jnp.bfloat16)
    video_self = query_ref[:, :, :VROWS, :].reshape(x_count * VTOK_DEV, HD)
    video_cross = query_ref[:, :, VROWS : 2 * VROWS, :].reshape(x_count * VTOK_DEV, HD)
    queries = (
        jnp.concatenate([video_self, audio_cross], axis=0),
        jnp.concatenate([video_cross, audio_self], axis=0),
    )
    pieces = (video_pieces, audio_pieces)
    biases = (video_bias_ref, audio_bias_ref)
    stats = []
    for kind in range(2):
        rows, stat = finish(*attend(queries[kind], pieces[kind], biases[kind]))
        stats.append(stat)
        start = kind * (VTOK_DEV + ATOK_DEV)
        for x in range(x_count):
            first = x * VTOK_DEV
            out_ref[x, start : start + VTOK_DEV, :] = rows[first : first + VTOK_DEV]
            first = x_count * VTOK_DEV + x * ATOK_DEV
            out_ref[x, start + VTOK_DEV : start + VTOK_DEV + ATOK_DEV, :] = rows[
                first : first + ATOK_DEV
            ]
    wide_stat, narrow_stat = VTOK_DEV // STATS_PER_ROW, ATOK_DEV // STATS_PER_ROW
    for x in range(x_count):
        picked = []
        for stat in stats:
            first = x * wide_stat
            picked.append(stat[first : first + wide_stat])
            first = x_count * wide_stat + x * narrow_stat
            picked.append(stat[first : first + narrow_stat])
        picked.append(jnp.zeros((STAT_ROWS - STAT_USED, HD), jnp.float32))
        out_ref[x, OUT_ROWS:, :] = jnp.concatenate(picked, axis=0).astype(jnp.bfloat16)


def combine_kernel(part_ref, gate_ref, out_ref):
    parts = part_ref.shape[0]
    in_place, _ = stat_places()
    source = lax.broadcasted_iota(jnp.int32, (HD, 2 * HD), 0) % STAT_FIELDS
    target = lax.broadcasted_iota(jnp.int32, (HD, 2 * HD), 1) // HD
    source = jnp.where(source < 3, (source + 1) // 2, 2)
    pick = jnp.where(source == target, 1.0, 0.0).astype(jnp.bfloat16)
    tokens = VTOK_DEV + ATOK_DEV
    for head in range(HEADS_HERE):
        cols = slice(head * HD, (head + 1) * HD)
        tops, totals = [], []
        for part in range(parts):
            rows = part_ref[part, OUT_ROWS:, cols].astype(jnp.float32)[:STAT_USED]
            rows = jnp.broadcast_to(
                rows[:, None, None, :], (STAT_USED, STATS_PER_ROW // 8, 8, HD)
            )
            rows = jnp.where(in_place, rows, 0.0).reshape(OUT_ROWS, HD)
            fields = jnp.dot(
                rows.astype(jnp.bfloat16), pick, preferred_element_type=jnp.float32
            )
            tops.append(fields[:, :HD])
            totals.append(fields[:, HD:])
        top = tops[0]
        for other in tops[1:]:
            top = jnp.maximum(top, other)
        shares = [jnp.exp2(t - top) * total for t, total in zip(tops, totals)]
        inverse = 1.0 / sum(shares)
        merged = sum(
            part_ref[part, :OUT_ROWS, cols].astype(jnp.float32) * (shares[part] * inverse)
            for part in range(parts)
        )
        video = merged[:VTOK_DEV] + gate_ref[0:1, cols] * merged[tokens : tokens + VTOK_DEV]
        audio = merged[tokens + VTOK_DEV :] + gate_ref[1:2, cols] * merged[VTOK_DEV:tokens]
        out_ref[:, :VROWS, cols] = video.reshape(RING, VROWS, HD).astype(jnp.bfloat16)
        for pair in range(RING // 2):
            rows = audio[pair * 8 : pair * 8 + 8].astype(jnp.bfloat16)
            out_ref[2 * pair, VROWS:, cols] = rows
            out_ref[2 * pair + 1, VROWS:, cols] = rows


def place_kernel(place_ref, back_ref, video_ref, audio_ref):
    core = place_ref[0]
    odd = place_ref[1]
    half_groups = RING // 2
    for j in range(half_groups):
        group = core * half_groups + j
        cols = slice(j * GROUP, (j + 1) * GROUP)
        for s in range(2):
            video_ref[s * VROWS : (s + 1) * VROWS, cols] = back_ref[s, group, :VROWS, :]
        first, second = (back_ref[s, group, VROWS:, :].astype(jnp.float32) for s in range(2))
        low = low_rows(first.shape)
        audio_ref[:, cols] = jnp.where(
            odd == 0,
            jnp.where(low, first, swap_halves(second)),
            jnp.where(low, swap_halves(first), second),
        ).astype(jnp.bfloat16)


def whole(memory_space=pltpu.VMEM):
    return pl.BlockSpec(memory_space=memory_space)


def params():
    return pltpu.CompilerParams(vmem_limit_bytes=VMEM_LIMIT)


def shards(
    video_proj,
    audio_proj,
    video_gains,
    audio_gains,
    cross_gates,
    timestep,
    video_counts,
    audio_counts,
):
    core = lax.axis_index("tp")
    x_count = lax.axis_size("x")
    z_index = lax.axis_index("z")
    parity = lax.axis_index("al")
    packed = pl.pallas_call(
        pack_kernel,
        grid=(1,),
        out_shape=jax.ShapeDtypeStruct((PACK_ROWS, D // 2), jnp.bfloat16),
        in_specs=[
            whole(pltpu.SMEM),
            pl.BlockSpec(video_proj.shape, lambda i: (0, 0, 0)),
            pl.BlockSpec(audio_proj.shape, lambda i: (0, 0, 0)),
            pl.BlockSpec(video_gains.shape, lambda i: (0, 0)),
            pl.BlockSpec(audio_gains.shape, lambda i: (0, 0)),
        ],
        out_specs=pl.BlockSpec((PACK_ROWS, D // 2), lambda i: (0, 0)),
        compiler_params=pltpu.CompilerParams(vmem_limit_bytes=PACK_VMEM),
        name="pack",
    )(core[None], video_proj, audio_proj, video_gains, audio_gains)
    packed = lax.all_gather(packed, "tp", axis=0)
    blocks = pl.pallas_call(
        norm_kernel,
        out_shape=jax.ShapeDtypeStruct((RING, 2 * BLOCK, GROUP), jnp.bfloat16),
        in_specs=[whole(pltpu.SMEM)] + [whole()] * 5,
        out_specs=whole(),
        compiler_params=params(),
        name="norm",
    )(core[None], video_proj, audio_proj, video_gains, audio_gains, packed)

    x_index = lax.axis_index("x")
    halves = jnp.stack([core, 1 - core])

    def allowed(counts):
        here = counts.reshape(YH, x_count, RING)
        return lax.dynamic_index_in_dim(here, x_index, 1, keepdims=False)

    def bias(live):
        return jnp.where(live, 0.0, MASKED).astype(jnp.float32).reshape(1, -1)

    allowed_video, allowed_audio = allowed(video_counts), allowed(audio_counts)
    biases = []
    for al in (parity, 1 - parity):
        aud = np.arange(AH) * AL + al
        video_first = (
            aud[None, :, None] * (2 * VROWS)
            + halves[:, None, None] * VROWS
            + np.arange(VROWS)[None, None, :]
        )
        audio_first = aud[:, None] * 8 + np.arange(8)[None, :]
        biases.append(
            (
                bias(video_first[:, None, :, None, :] < allowed_video[None, :, None, :, None]),
                bias(audio_first[None, :, None, :] < allowed_audio[:, None, :, None]),
            )
        )
    places = jnp.stack([core, z_index % 2])
    gates = lax.dynamic_index_in_dim(cross_gates, timestep[0], 1, keepdims=False)
    gates, packed = lax.optimization_barrier((gates, packed))
    gates = lax.all_gather(gates, "tp", axis=0)
    gates = lax.dynamic_slice(
        gates,
        (z_index // (RING // 2), 0, (z_index % (RING // 2)) * GROUP),
        (1, 2, GROUP),
    )[0].astype(jnp.float32)
    blocks = lax.all_to_all(blocks, "z", split_axis=0, concat_axis=0)
    keyval, queries = blocks[:, :BLOCK], blocks[:, BLOCK:]
    biases = [jnp.concatenate(part, axis=1) for part in zip(*biases)]
    keyval, queries, gates, biases, places = lax.optimization_barrier(
        (keyval, queries, gates, biases, places)
    )
    keyval = lax.all_gather(keyval, ("yh", "ah"), axis=0, tiled=True)
    keyval, queries = lax.optimization_barrier((keyval, queries))
    queries = lax.all_gather(queries, "x", axis=0)
    full_shape = (YH, AH, RING, BLOCK, GROUP)

    y_count = YH * AH * AL
    ways = [
        (y * 2 + c, (y + 1 - 2 * c) % y_count * 2 + c) for y in range(y_count) for c in range(2)
    ]
    swap = [(0, 1), (1, 0)]
    far = lax.ppermute(keyval, ("yh", "ah", "al", "tp"), ways)
    keyval_other = lax.ppermute(keyval, "tp", swap)
    far, queries = lax.optimization_barrier((far, queries))
    far_other = lax.ppermute(far, "tp", swap)
    near = [keyval.reshape(full_shape), keyval_other.reshape(full_shape)]
    far = [far.reshape(full_shape), far_other.reshape(full_shape)]

    keyval_spec = pl.BlockSpec(full_shape[:-1] + (HD,), lambda h: (0, 0, 0, 0, h))
    partial = pl.pallas_call(
        attend_kernel,
        grid=(HEADS_HERE,),
        out_shape=jax.ShapeDtypeStruct(
            (x_count, OUT_ROWS + STAT_ROWS, GROUP), jnp.bfloat16
        ),
        in_specs=[
            whole(pltpu.SMEM),
            pl.BlockSpec((x_count, RING, BLOCK, HD), lambda h: (0, 0, 0, h)),
            *[keyval_spec] * 4,
            *[pl.BlockSpec(bias.shape, lambda h: (0, 0)) for bias in biases],
        ],
        out_specs=pl.BlockSpec((x_count, OUT_ROWS + STAT_ROWS, HD), lambda h: (0, 0, h)),
        compiler_params=params(),
        name="attend",
    )(core[None], queries, *near, *far, *biases)
    partial = lax.all_to_all(partial, "x", split_axis=0, concat_axis=0)
    back = pl.pallas_call(
        combine_kernel,
        out_shape=jax.ShapeDtypeStruct((RING, BACK_ROWS, GROUP), jnp.bfloat16),
        in_specs=[whole(), whole()],
        out_specs=whole(),
        compiler_params=params(),
        name="combine",
    )(partial, gates)
    back = lax.all_to_all(back, "z", split_axis=0, concat_axis=0)
    back = lax.all_gather(back, "tp", axis=0)
    return pl.pallas_call(
        place_kernel,
        out_shape=(
            jax.ShapeDtypeStruct((2 * VROWS, D // 2), jnp.bfloat16),
            jax.ShapeDtypeStruct((2 * AROWS, D // 2), jnp.bfloat16),
        ),
        in_specs=[whole(pltpu.SMEM), whole()],
        out_specs=(whole(), whole()),
        compiler_params=params(),
        name="place",
    )(places, back)


def solution(mesh):
    vid = mesh.devices.shape[0]
    cut = (YH, vid // (YH * RING), RING, AH, AL, 2)
    axes = ("yh", "x", "z", "ah", "al", "tp")
    fine = Mesh(mesh.devices.reshape(cut), axes)
    tokens = axes[:-1]
    in_specs = (
        P(None, tokens, "tp"),
        P(None, tokens, "tp"),
        P(None, "tp"),
        P(None, "tp"),
        P(None, None, "tp"),
        P(),
        P(),
        P(),
    )
    out_specs = (P(tokens, "tp"), P(tokens, "tp"))
    return jax.shard_map(
        shards, mesh=fine, in_specs=in_specs, out_specs=out_specs, check_vma=False
    )
```

```python
import math

import jax
import jax.numpy as jnp
import numpy as np
from jax import lax
from jax.experimental import pallas as pl
from jax.experimental.pallas import tpu as pltpu
from jax.sharding import Mesh
from jax.sharding import PartitionSpec as P

D = 3072
HD = 128
VTOK_DEV = 128
ATOK_DEV = 32
EPSILON = 1e-06
MASKED = -1e30

YH = 2
AH = 2
AL = 2
RING = 8
GROUP = D // RING
HEADS_HERE = GROUP // HD
VROWS = 16
AROWS = 4
BLOCK = 2 * VROWS + 2 * AROWS
OUT_ROWS = 2 * (VTOK_DEV + ATOK_DEV)
STAT_FIELDS = 4
STATS_PER_ROW = HD // STAT_FIELDS
STAT_USED = OUT_ROWS // STATS_PER_ROW
STAT_ROWS = 16
BACK_ROWS = VROWS + 8
AUDIO_ROW = 4 * VROWS
SMALL_ROW = AUDIO_ROW + 4 * 2 * AROWS
PACK_ROWS = SMALL_ROW + 32
KEY_STEP = 256
SCORE_SCALE = HD ** (-0.5) * math.log2(math.e)
VMEM_LIMIT = 48 * 1024 * 1024
PACK_VMEM = 60 * 1024 * 1024


def low_rows(shape):
    return lax.broadcasted_iota(jnp.int32, shape, len(shape) - 2) % 8 < 4


def swap_halves(rows):
    return pltpu.roll(rows, 4, axis=rows.ndim - 2)


def pack_kernel(core_ref, video_ref, audio_ref, video_gains_ref, audio_gains_ref, out_ref):
    first = pl.multiple_of((1 - core_ref[0]) * VROWS, VROWS)
    for array in range(4):
        row = array * VROWS
        out_ref[row : row + VROWS, :] = video_ref[array, pl.ds(first, VROWS), :]
        row = AUDIO_ROW + array * 8
        out_ref[row : row + 8, :] = audio_ref[array]
    gains = [video_gains_ref[...], audio_gains_ref[...]]
    rest = jnp.concatenate(gains + [jnp.zeros_like(gains[0][:2])], axis=0)
    pieces = []
    for _ in range(3):
        piece = rest.astype(jnp.bfloat16).astype(jnp.float32)
        pieces.append(piece)
        rest = rest - piece
    pieces.append(jnp.zeros_like(rest))
    out_ref[SMALL_ROW:, :] = jnp.concatenate(pieces, axis=0).astype(jnp.bfloat16)


def norm_kernel(
    core_ref,
    video_ref,
    audio_ref,
    video_gains_ref,
    audio_gains_ref,
    packed_ref,
    out_ref,
):
    core = core_ref[0]
    at_zero = core == 0
    own_first = pl.multiple_of(core * VROWS, VROWS)
    small = packed_ref[1 - core, SMALL_ROW:, :].astype(jnp.float32)
    other_gains = small[0:8] + small[8:16] + small[16:24]
    own_gains = jnp.concatenate([video_gains_ref[...], audio_gains_ref[...]], axis=0)

    def ordered(own, other):
        return [jnp.where(at_zero, own, other), jnp.where(at_zero, other, own)]

    gains = ordered(own_gains, other_gains[:6])
    half_groups = RING // 2

    def normed(halves, gain_row, extra):
        total = sum(jnp.sum(v * v, axis=1, keepdims=True) for v in halves)
        inverse = lax.rsqrt(total / D + EPSILON)
        return [
            v * inverse * (gains[s][gain_row : gain_row + 1, :] * extra)
            for s, v in enumerate(halves)
        ]

    def spread(row, halves):
        count = halves[0].shape[0]
        for group in range(RING):
            col = (group % half_groups) * GROUP
            out_ref[group, row : row + count, :] = halves[group // half_groups][
                :, col : col + GROUP
            ].astype(jnp.bfloat16)

    def video(array):
        first = array * VROWS
        return ordered(
            video_ref[array, pl.ds(own_first, VROWS), :].astype(jnp.float32),
            packed_ref[1 - core, first : first + VROWS, :].astype(jnp.float32),
        )

    def audio(array):
        first = AUDIO_ROW + array * 8
        return ordered(
            audio_ref[array].astype(jnp.float32),
            packed_ref[1 - core, first : first + 8, :].astype(jnp.float32),
        )

    spread(0, normed(video(2), 2, 1.0))
    spread(VROWS, video(3))
    audio_key = normed(audio(2), 5, 1.0)
    audio_value = audio(3)
    spread(
        2 * VROWS,
        [jnp.where(at_zero, k, v) for k, v in zip(audio_key, audio_value)],
    )
    spread(BLOCK, normed(video(0), 0, SCORE_SCALE))
    spread(BLOCK + VROWS, normed(video(1), 1, SCORE_SCALE))
    audio_self = normed(audio(0), 3, SCORE_SCALE)
    audio_cross = normed(audio(1), 4, SCORE_SCALE)
    mixed = []
    for own, other in zip(audio_self, audio_cross):
        low = low_rows(own.shape)
        mixed.append(
            jnp.where(
                at_zero,
                jnp.where(low, own, swap_halves(other)),
                jnp.where(low, swap_halves(own), other),
            )
        )
    spread(BLOCK + 2 * VROWS, mixed)


def stat_places():
    shape = (1, STATS_PER_ROW // 8, 8, HD)
    tile, row, lane = (lax.broadcasted_iota(jnp.int32, shape, i) for i in (1, 2, 3))
    return lane // STAT_FIELDS == tile * 8 + row, lane % STAT_FIELDS


def attend_kernel(core_ref, query_ref, *refs):
    x_count = query_ref.shape[0]
    *keyval_refs, video_bias_ref, audio_bias_ref, out_ref = refs
    holds_keys = core_ref[0] == 0

    def rows_of(ref, first, last):
        rows = ref[:, :, :, first:last, :]
        if last - first == 8:
            rows = rows.astype(jnp.float32)
        return rows.reshape(-1, HD)

    video_pieces, audio_pieces = [], []
    for own, other in zip(keyval_refs[::2], keyval_refs[1::2]):
        for ref in (own, other):
            key = rows_of(ref, 0, VROWS)
            value = rows_of(ref, VROWS, 2 * VROWS)
            for first in range(0, key.shape[0], KEY_STEP):
                keys = slice(first, first + KEY_STEP)
                video_pieces.append((key[keys], value[keys]))
        own, other = (rows_of(ref, 2 * VROWS, BLOCK) for ref in (own, other))
        audio_pieces.append(
            (
                jnp.where(holds_keys, own, other).astype(jnp.bfloat16),
                jnp.where(holds_keys, other, own).astype(jnp.bfloat16),
            )
        )
    in_place, field = stat_places()

    def attend(queries, pieces, bias_ref):
        state, first = None, 0
        for key, value in pieces:
            keys = slice(first, first + key.shape[0])
            first = keys.stop
            scores = lax.dot_general(
                queries, key, (((1,), (1,)), ((), ())), preferred_element_type=jnp.float32
            )
            scores = scores + bias_ref[0:1, keys]
            top = jnp.max(scores, axis=1, keepdims=True)
            top = top.astype(jnp.bfloat16).astype(jnp.float32)
            if state is not None:
                top = jnp.maximum(top, state[0])
            weights = jnp.exp2(scores - top)
            total = sum(weights[:, i : i + HD] for i in range(0, weights.shape[1], HD))
            sums = jnp.dot(
                weights.astype(jnp.bfloat16), value, preferred_element_type=jnp.float32
            )
            if state is not None:
                keep = jnp.exp2(state[0] - top)
                total = total + state[1] * keep
                sums = sums + state[2] * keep
            state = top, total, sums
        top, total, sums = state
        return top, jnp.sum(total, axis=1, keepdims=True), sums

    def finish(top, total, sums):
        high = total.astype(jnp.bfloat16).astype(jnp.float32)

        def wide(column):
            wide_column = jnp.broadcast_to(column, (column.shape[0], HD))
            return wide_column.reshape(-1, STATS_PER_ROW // 8, 8, HD)

        stats = jnp.where(
            field == 0,
            wide(top),
            jnp.where(field == 1, wide(high), wide(total - high)),
        )
        stats = jnp.sum(jnp.where(in_place & (field < 3), stats, 0.0), axis=(1, 2))
        return (sums * (1.0 / total)).astype(jnp.bfloat16), stats

    audio_rows = query_ref[:, :, 2 * VROWS :, :].astype(jnp.float32)
    audio_rows = audio_rows.reshape(x_count * RING // 2, 2, 8, HD)
    even, odd = audio_rows[:, 0], audio_rows[:, 1]
    low = low_rows(even.shape)
    audio_self = jnp.where(low, even, swap_halves(odd)).reshape(-1, HD).astype(jnp.bfloat16)
    audio_cross = jnp.where(low, swap_halves(even), odd).reshape(-1, HD).astype(jnp.bfloat16)
    video_self = query_ref[:, :, :VROWS, :].reshape(x_count * VTOK_DEV, HD)
    video_cross = query_ref[:, :, VROWS : 2 * VROWS, :].reshape(x_count * VTOK_DEV, HD)
    queries = (
        jnp.concatenate([video_self, audio_cross], axis=0),
        jnp.concatenate([video_cross, audio_self], axis=0),
    )
    pieces = (video_pieces, audio_pieces)
    biases = (video_bias_ref, audio_bias_ref)
    stats = []
    for kind in range(2):
        rows, stat = finish(*attend(queries[kind], pieces[kind], biases[kind]))
        stats.append(stat)
        start = kind * (VTOK_DEV + ATOK_DEV)
        for x in range(x_count):
            first = x * VTOK_DEV
            out_ref[x, start : start + VTOK_DEV, :] = rows[first : first + VTOK_DEV]
            first = x_count * VTOK_DEV + x * ATOK_DEV
            out_ref[x, start + VTOK_DEV : start + VTOK_DEV + ATOK_DEV, :] = rows[
                first : first + ATOK_DEV
            ]
    wide_stat, narrow_stat = VTOK_DEV // STATS_PER_ROW, ATOK_DEV // STATS_PER_ROW
    for x in range(x_count):
        picked = []
        for stat in stats:
            first = x * wide_stat
            picked.append(stat[first : first + wide_stat])
            first = x_count * wide_stat + x * narrow_stat
            picked.append(stat[first : first + narrow_stat])
        picked.append(jnp.zeros((STAT_ROWS - STAT_USED, HD), jnp.float32))
        out_ref[x, OUT_ROWS:, :] = jnp.concatenate(picked, axis=0).astype(jnp.bfloat16)


def combine_kernel(part_ref, gate_ref, out_ref):
    parts = part_ref.shape[0]
    in_place, _ = stat_places()
    source = lax.broadcasted_iota(jnp.int32, (HD, 2 * HD), 0) % STAT_FIELDS
    target = lax.broadcasted_iota(jnp.int32, (HD, 2 * HD), 1) // HD
    source = jnp.where(source < 3, (source + 1) // 2, 2)
    pick = jnp.where(source == target, 1.0, 0.0).astype(jnp.bfloat16)
    tokens = VTOK_DEV + ATOK_DEV
    for head in range(HEADS_HERE):
        cols = slice(head * HD, (head + 1) * HD)
        tops, totals = [], []
        for part in range(parts):
            rows = part_ref[part, OUT_ROWS:, cols].astype(jnp.float32)[:STAT_USED]
            rows = jnp.broadcast_to(
                rows[:, None, None, :], (STAT_USED, STATS_PER_ROW // 8, 8, HD)
            )
            rows = jnp.where(in_place, rows, 0.0).reshape(OUT_ROWS, HD)
            fields = jnp.dot(
                rows.astype(jnp.bfloat16), pick, preferred_element_type=jnp.float32
            )
            tops.append(fields[:, :HD])
            totals.append(fields[:, HD:])
        top = tops[0]
        for other in tops[1:]:
            top = jnp.maximum(top, other)
        shares = [jnp.exp2(t - top) * total for t, total in zip(tops, totals)]
        inverse = 1.0 / sum(shares)
        merged = sum(
            part_ref[part, :OUT_ROWS, cols].astype(jnp.float32) * (shares[part] * inverse)
            for part in range(parts)
        )
        video = merged[:VTOK_DEV] + gate_ref[0:1, cols] * merged[tokens : tokens + VTOK_DEV]
        audio = merged[tokens + VTOK_DEV :] + gate_ref[1:2, cols] * merged[VTOK_DEV:tokens]
        out_ref[:, :VROWS, cols] = video.reshape(RING, VROWS, HD).astype(jnp.bfloat16)
        for pair in range(RING // 2):
            rows = audio[pair * 8 : pair * 8 + 8].astype(jnp.bfloat16)
            out_ref[2 * pair, VROWS:, cols] = rows
            out_ref[2 * pair + 1, VROWS:, cols] = rows


def place_kernel(place_ref, back_ref, video_ref, audio_ref):
    core = place_ref[0]
    odd = place_ref[1]
    half_groups = RING // 2
    for j in range(half_groups):
        group = core * half_groups + j
        cols = slice(j * GROUP, (j + 1) * GROUP)
        for s in range(2):
            video_ref[s * VROWS : (s + 1) * VROWS, cols] = back_ref[s, group, :VROWS, :]
        first, second = (back_ref[s, group, VROWS:, :].astype(jnp.float32) for s in range(2))
        low = low_rows(first.shape)
        audio_ref[:, cols] = jnp.where(
            odd == 0,
            jnp.where(low, first, swap_halves(second)),
            jnp.where(low, swap_halves(first), second),
        ).astype(jnp.bfloat16)


def whole(memory_space=pltpu.VMEM):
    return pl.BlockSpec(memory_space=memory_space)


def params():
    return pltpu.CompilerParams(vmem_limit_bytes=VMEM_LIMIT)


def shards(
    video_proj,
    audio_proj,
    video_gains,
    audio_gains,
    cross_gates,
    timestep,
    video_counts,
    audio_counts,
):
    core = lax.axis_index("tp")
    x_count = lax.axis_size("x")
    z_index = lax.axis_index("z")
    parity = lax.axis_index("al")
    packed = pl.pallas_call(
        pack_kernel,
        grid=(1,),
        out_shape=jax.ShapeDtypeStruct((PACK_ROWS, D // 2), jnp.bfloat16),
        in_specs=[
            whole(pltpu.SMEM),
            pl.BlockSpec(video_proj.shape, lambda i: (0, 0, 0)),
            pl.BlockSpec(audio_proj.shape, lambda i: (0, 0, 0)),
            pl.BlockSpec(video_gains.shape, lambda i: (0, 0)),
            pl.BlockSpec(audio_gains.shape, lambda i: (0, 0)),
        ],
        out_specs=pl.BlockSpec((PACK_ROWS, D // 2), lambda i: (0, 0)),
        compiler_params=pltpu.CompilerParams(vmem_limit_bytes=PACK_VMEM),
        name="pack",
    )(core[None], video_proj, audio_proj, video_gains, audio_gains)
    packed = lax.all_gather(packed, "tp", axis=0)
    blocks = pl.pallas_call(
        norm_kernel,
        out_shape=jax.ShapeDtypeStruct((RING, 2 * BLOCK, GROUP), jnp.bfloat16),
        in_specs=[whole(pltpu.SMEM)] + [whole()] * 5,
        out_specs=whole(),
        compiler_params=params(),
        name="norm",
    )(core[None], video_proj, audio_proj, video_gains, audio_gains, packed)

    x_index = lax.axis_index("x")
    halves = jnp.stack([core, 1 - core])

    def allowed(counts):
        here = counts.reshape(YH, x_count, RING)
        return lax.dynamic_index_in_dim(here, x_index, 1, keepdims=False)

    def bias(live):
        return jnp.where(live, 0.0, MASKED).astype(jnp.float32).reshape(1, -1)

    allowed_video, allowed_audio = allowed(video_counts), allowed(audio_counts)
    biases = []
    for al in (parity, 1 - parity):
        aud = np.arange(AH) * AL + al
        video_first = (
            aud[None, :, None] * (2 * VROWS)
            + halves[:, None, None] * VROWS
            + np.arange(VROWS)[None, None, :]
        )
        audio_first = aud[:, None] * 8 + np.arange(8)[None, :]
        biases.append(
            (
                bias(video_first[:, None, :, None, :] < allowed_video[None, :, None, :, None]),
                bias(audio_first[None, :, None, :] < allowed_audio[:, None, :, None]),
            )
        )
    places = jnp.stack([core, z_index % 2])
    gates = lax.dynamic_index_in_dim(cross_gates, timestep[0], 1, keepdims=False)
    gates, packed = lax.optimization_barrier((gates, packed))
    gates = lax.all_gather(gates, "tp", axis=0)
    gates = lax.dynamic_slice(
        gates,
        (z_index // (RING // 2), 0, (z_index % (RING // 2)) * GROUP),
        (1, 2, GROUP),
    )[0].astype(jnp.float32)
    blocks = lax.all_to_all(blocks, "z", split_axis=0, concat_axis=0)
    keyval, queries = blocks[:, :BLOCK], blocks[:, BLOCK:]
    biases = [jnp.concatenate(part, axis=1) for part in zip(*biases)]
    keyval, queries, gates, biases, places = lax.optimization_barrier(
        (keyval, queries, gates, biases, places)
    )
    keyval = lax.all_gather(keyval, ("yh", "ah"), axis=0, tiled=True)
    keyval, queries = lax.optimization_barrier((keyval, queries))
    queries = lax.all_gather(queries, "x", axis=0)
    full_shape = (YH, AH, RING, BLOCK, GROUP)

    y_count = YH * AH * AL
    ways = [
        (y * 2 + c, (y + 1 - 2 * c) % y_count * 2 + c) for y in range(y_count) for c in range(2)
    ]
    swap = [(0, 1), (1, 0)]
    far = lax.ppermute(keyval, ("yh", "ah", "al", "tp"), ways)
    near, queries = lax.optimization_barrier((keyval, queries))
    keyval_other = lax.ppermute(near, "tp", swap)
    far, queries = lax.optimization_barrier((far, queries))
    far_other = lax.ppermute(far, "tp", swap)
    near = [keyval.reshape(full_shape), keyval_other.reshape(full_shape)]
    far = [far.reshape(full_shape), far_other.reshape(full_shape)]

    keyval_spec = pl.BlockSpec(full_shape[:-1] + (HD,), lambda h: (0, 0, 0, 0, h))
    partial = pl.pallas_call(
        attend_kernel,
        grid=(HEADS_HERE,),
        out_shape=jax.ShapeDtypeStruct(
            (x_count, OUT_ROWS + STAT_ROWS, GROUP), jnp.bfloat16
        ),
        in_specs=[
            whole(pltpu.SMEM),
            pl.BlockSpec((x_count, RING, BLOCK, HD), lambda h: (0, 0, 0, h)),
            *[keyval_spec] * 4,
            *[pl.BlockSpec(bias.shape, lambda h: (0, 0)) for bias in biases],
        ],
        out_specs=pl.BlockSpec((x_count, OUT_ROWS + STAT_ROWS, HD), lambda h: (0, 0, h)),
        compiler_params=params(),
        name="attend",
    )(core[None], queries, *near, *far, *biases)
    partial = lax.all_to_all(partial, "x", split_axis=0, concat_axis=0)
    back = pl.pallas_call(
        combine_kernel,
        out_shape=jax.ShapeDtypeStruct((RING, BACK_ROWS, GROUP), jnp.bfloat16),
        in_specs=[whole(), whole()],
        out_specs=whole(),
        compiler_params=params(),
        name="combine",
    )(partial, gates)
    back = lax.all_to_all(back, "z", split_axis=0, concat_axis=0)
    back = lax.all_gather(back, "tp", axis=0)
    return pl.pallas_call(
        place_kernel,
        out_shape=(
            jax.ShapeDtypeStruct((2 * VROWS, D // 2), jnp.bfloat16),
            jax.ShapeDtypeStruct((2 * AROWS, D // 2), jnp.bfloat16),
        ),
        in_specs=[whole(pltpu.SMEM), whole()],
        out_specs=(whole(), whole()),
        compiler_params=params(),
        name="place",
    )(places, back)


def solution(mesh):
    vid = mesh.devices.shape[0]
    cut = (YH, vid // (YH * RING), RING, AH, AL, 2)
    axes = ("yh", "x", "z", "ah", "al", "tp")
    fine = Mesh(mesh.devices.reshape(cut), axes)
    tokens = axes[:-1]
    in_specs = (
        P(None, tokens, "tp"),
        P(None, tokens, "tp"),
        P(None, "tp"),
        P(None, "tp"),
        P(None, None, "tp"),
        P(),
        P(),
        P(),
    )
    out_specs = (P(tokens, "tp"), P(tokens, "tp"))
    return jax.shard_map(
        shards, mesh=fine, in_specs=in_specs, out_specs=out_specs, check_vma=False
    )
```

```python
import math

import jax
import jax.numpy as jnp
import numpy as np
from jax import lax
from jax.experimental import pallas as pl
from jax.experimental.pallas import tpu as pltpu
from jax.sharding import Mesh
from jax.sharding import PartitionSpec as P

D = 3072
HD = 128
VTOK_DEV = 128
ATOK_DEV = 32
EPSILON = 1e-06
MASKED = -1e30

YH = 2
AH = 2
AL = 2
RING = 8
GROUP = D // RING
HEADS_HERE = GROUP // HD
VROWS = 16
AROWS = 4
BLOCK = 2 * VROWS + 2 * AROWS
OUT_ROWS = 2 * (VTOK_DEV + ATOK_DEV)
STAT_FIELDS = 4
STATS_PER_ROW = HD // STAT_FIELDS
STAT_USED = OUT_ROWS // STATS_PER_ROW
STAT_ROWS = 16
BACK_ROWS = VROWS + 8
AUDIO_ROW = 4 * VROWS
SMALL_ROW = AUDIO_ROW + 4 * 2 * AROWS
PACK_ROWS = SMALL_ROW + 32
KEY_STEP = 512
SCORE_SCALE = HD ** (-0.5) * math.log2(math.e)
VMEM_LIMIT = 48 * 1024 * 1024
PACK_VMEM = 60 * 1024 * 1024


def low_rows(shape):
    return lax.broadcasted_iota(jnp.int32, shape, len(shape) - 2) % 8 < 4


def swap_halves(rows):
    return pltpu.roll(rows, 4, axis=rows.ndim - 2)


def pack_kernel(core_ref, video_ref, audio_ref, video_gains_ref, audio_gains_ref, out_ref):
    first = pl.multiple_of((1 - core_ref[0]) * VROWS, VROWS)
    for array in range(4):
        row = array * VROWS
        out_ref[row : row + VROWS, :] = video_ref[array, pl.ds(first, VROWS), :]
        row = AUDIO_ROW + array * 8
        out_ref[row : row + 8, :] = audio_ref[array]
    gains = [video_gains_ref[...], audio_gains_ref[...]]
    rest = jnp.concatenate(gains + [jnp.zeros_like(gains[0][:2])], axis=0)
    pieces = []
    for _ in range(3):
        piece = rest.astype(jnp.bfloat16).astype(jnp.float32)
        pieces.append(piece)
        rest = rest - piece
    pieces.append(jnp.zeros_like(rest))
    out_ref[SMALL_ROW:, :] = jnp.concatenate(pieces, axis=0).astype(jnp.bfloat16)


def norm_kernel(
    core_ref,
    video_ref,
    audio_ref,
    video_gains_ref,
    audio_gains_ref,
    packed_ref,
    out_ref,
):
    core = core_ref[0]
    at_zero = core == 0
    own_first = pl.multiple_of(core * VROWS, VROWS)
    small = packed_ref[1 - core, SMALL_ROW:, :].astype(jnp.float32)
    other_gains = small[0:8] + small[8:16] + small[16:24]
    own_gains = jnp.concatenate([video_gains_ref[...], audio_gains_ref[...]], axis=0)

    def ordered(own, other):
        return [jnp.where(at_zero, own, other), jnp.where(at_zero, other, own)]

    gains = ordered(own_gains, other_gains[:6])
    half_groups = RING // 2

    def normed(halves, gain_row, extra):
        total = sum(jnp.sum(v * v, axis=1, keepdims=True) for v in halves)
        inverse = lax.rsqrt(total / D + EPSILON)
        return [
            v * inverse * (gains[s][gain_row : gain_row + 1, :] * extra)
            for s, v in enumerate(halves)
        ]

    def spread(row, halves):
        count = halves[0].shape[0]
        for group in range(RING):
            col = (group % half_groups) * GROUP
            out_ref[group, row : row + count, :] = halves[group // half_groups][
                :, col : col + GROUP
            ].astype(jnp.bfloat16)

    def video(array):
        first = array * VROWS
        return ordered(
            video_ref[array, pl.ds(own_first, VROWS), :].astype(jnp.float32),
            packed_ref[1 - core, first : first + VROWS, :].astype(jnp.float32),
        )

    def audio(array):
        first = AUDIO_ROW + array * 8
        return ordered(
            audio_ref[array].astype(jnp.float32),
            packed_ref[1 - core, first : first + 8, :].astype(jnp.float32),
        )

    spread(0, normed(video(2), 2, 1.0))
    spread(VROWS, video(3))
    audio_key = normed(audio(2), 5, 1.0)
    audio_value = audio(3)
    spread(
        2 * VROWS,
        [jnp.where(at_zero, k, v) for k, v in zip(audio_key, audio_value)],
    )
    spread(BLOCK, normed(video(0), 0, SCORE_SCALE))
    spread(BLOCK + VROWS, normed(video(1), 1, SCORE_SCALE))
    audio_self = normed(audio(0), 3, SCORE_SCALE)
    audio_cross = normed(audio(1), 4, SCORE_SCALE)
    mixed = []
    for own, other in zip(audio_self, audio_cross):
        low = low_rows(own.shape)
        mixed.append(
            jnp.where(
                at_zero,
                jnp.where(low, own, swap_halves(other)),
                jnp.where(low, swap_halves(own), other),
            )
        )
    spread(BLOCK + 2 * VROWS, mixed)


def stat_places():
    shape = (1, STATS_PER_ROW // 8, 8, HD)
    tile, row, lane = (lax.broadcasted_iota(jnp.int32, shape, i) for i in (1, 2, 3))
    return lane // STAT_FIELDS == tile * 8 + row, lane % STAT_FIELDS


def attend_kernel(core_ref, query_ref, *refs):
    x_count = query_ref.shape[0]
    *keyval_refs, video_bias_ref, audio_bias_ref, out_ref = refs
    holds_keys = core_ref[0] == 0

    def rows_of(ref, first, last):
        rows = ref[:, :, :, first:last, :]
        if last - first == 8:
            rows = rows.astype(jnp.float32)
        return rows.reshape(-1, HD)

    video_pieces, audio_pieces = [], []
    for own, other in zip(keyval_refs[::2], keyval_refs[1::2]):
        for ref in (own, other):
            key = rows_of(ref, 0, VROWS)
            value = rows_of(ref, VROWS, 2 * VROWS)
            for first in range(0, key.shape[0], KEY_STEP):
                keys = slice(first, first + KEY_STEP)
                video_pieces.append((key[keys], value[keys]))
        own, other = (rows_of(ref, 2 * VROWS, BLOCK) for ref in (own, other))
        audio_pieces.append(
            (
                jnp.where(holds_keys, own, other).astype(jnp.bfloat16),
                jnp.where(holds_keys, other, own).astype(jnp.bfloat16),
            )
        )
    in_place, field = stat_places()

    def attend(queries, pieces, bias_ref):
        state, first = None, 0
        for key, value in pieces:
            keys = slice(first, first + key.shape[0])
            first = keys.stop
            scores = lax.dot_general(
                queries, key, (((1,), (1,)), ((), ())), preferred_element_type=jnp.float32
            )
            scores = scores + bias_ref[0:1, keys]
            top = jnp.max(scores, axis=1, keepdims=True)
            top = top.astype(jnp.bfloat16).astype(jnp.float32)
            if state is not None:
                top = jnp.maximum(top, state[0])
            weights = jnp.exp2(scores - top)
            total = sum(weights[:, i : i + HD] for i in range(0, weights.shape[1], HD))
            sums = jnp.dot(
                weights.astype(jnp.bfloat16), value, preferred_element_type=jnp.float32
            )
            if state is not None:
                keep = jnp.exp2(state[0] - top)
                total = total + state[1] * keep
                sums = sums + state[2] * keep
            state = top, total, sums
        top, total, sums = state
        return top, jnp.sum(total, axis=1, keepdims=True), sums

    def finish(top, total, sums):
        high = total.astype(jnp.bfloat16).astype(jnp.float32)

        def wide(column):
            wide_column = jnp.broadcast_to(column, (column.shape[0], HD))
            return wide_column.reshape(-1, STATS_PER_ROW // 8, 8, HD)

        stats = jnp.where(
            field == 0,
            wide(top),
            jnp.where(field == 1, wide(high), wide(total - high)),
        )
        stats = jnp.sum(jnp.where(in_place & (field < 3), stats, 0.0), axis=(1, 2))
        return (sums * (1.0 / total)).astype(jnp.bfloat16), stats

    audio_rows = query_ref[:, :, 2 * VROWS :, :].astype(jnp.float32)
    audio_rows = audio_rows.reshape(x_count * RING // 2, 2, 8, HD)
    even, odd = audio_rows[:, 0], audio_rows[:, 1]
    low = low_rows(even.shape)
    audio_self = jnp.where(low, even, swap_halves(odd)).reshape(-1, HD).astype(jnp.bfloat16)
    audio_cross = jnp.where(low, swap_halves(even), odd).reshape(-1, HD).astype(jnp.bfloat16)
    video_self = query_ref[:, :, :VROWS, :].reshape(x_count * VTOK_DEV, HD)
    video_cross = query_ref[:, :, VROWS : 2 * VROWS, :].reshape(x_count * VTOK_DEV, HD)
    queries = (
        jnp.concatenate([video_self, audio_cross], axis=0),
        jnp.concatenate([video_cross, audio_self], axis=0),
    )
    pieces = (video_pieces, audio_pieces)
    biases = (video_bias_ref, audio_bias_ref)
    stats = []
    for kind in range(2):
        rows, stat = finish(*attend(queries[kind], pieces[kind], biases[kind]))
        stats.append(stat)
        start = kind * (VTOK_DEV + ATOK_DEV)
        for x in range(x_count):
            first = x * VTOK_DEV
            out_ref[x, start : start + VTOK_DEV, :] = rows[first : first + VTOK_DEV]
            first = x_count * VTOK_DEV + x * ATOK_DEV
            out_ref[x, start + VTOK_DEV : start + VTOK_DEV + ATOK_DEV, :] = rows[
                first : first + ATOK_DEV
            ]
    wide_stat, narrow_stat = VTOK_DEV // STATS_PER_ROW, ATOK_DEV // STATS_PER_ROW
    for x in range(x_count):
        picked = []
        for stat in stats:
            first = x * wide_stat
            picked.append(stat[first : first + wide_stat])
            first = x_count * wide_stat + x * narrow_stat
            picked.append(stat[first : first + narrow_stat])
        picked.append(jnp.zeros((STAT_ROWS - STAT_USED, HD), jnp.float32))
        out_ref[x, OUT_ROWS:, :] = jnp.concatenate(picked, axis=0).astype(jnp.bfloat16)


def combine_kernel(part_ref, gate_ref, out_ref):
    parts = part_ref.shape[0]
    in_place, _ = stat_places()
    source = lax.broadcasted_iota(jnp.int32, (HD, 2 * HD), 0) % STAT_FIELDS
    target = lax.broadcasted_iota(jnp.int32, (HD, 2 * HD), 1) // HD
    source = jnp.where(source < 3, (source + 1) // 2, 2)
    pick = jnp.where(source == target, 1.0, 0.0).astype(jnp.bfloat16)
    tokens = VTOK_DEV + ATOK_DEV
    for head in range(HEADS_HERE):
        cols = slice(head * HD, (head + 1) * HD)
        tops, totals = [], []
        for part in range(parts):
            rows = part_ref[part, OUT_ROWS:, cols].astype(jnp.float32)[:STAT_USED]
            rows = jnp.broadcast_to(
                rows[:, None, None, :], (STAT_USED, STATS_PER_ROW // 8, 8, HD)
            )
            rows = jnp.where(in_place, rows, 0.0).reshape(OUT_ROWS, HD)
            fields = jnp.dot(
                rows.astype(jnp.bfloat16), pick, preferred_element_type=jnp.float32
            )
            tops.append(fields[:, :HD])
            totals.append(fields[:, HD:])
        top = tops[0]
        for other in tops[1:]:
            top = jnp.maximum(top, other)
        shares = [jnp.exp2(t - top) * total for t, total in zip(tops, totals)]
        inverse = 1.0 / sum(shares)
        merged = sum(
            part_ref[part, :OUT_ROWS, cols].astype(jnp.float32) * (shares[part] * inverse)
            for part in range(parts)
        )
        video = merged[:VTOK_DEV] + gate_ref[0:1, cols] * merged[tokens : tokens + VTOK_DEV]
        audio = merged[tokens + VTOK_DEV :] + gate_ref[1:2, cols] * merged[VTOK_DEV:tokens]
        out_ref[:, :VROWS, cols] = video.reshape(RING, VROWS, HD).astype(jnp.bfloat16)
        for pair in range(RING // 2):
            rows = audio[pair * 8 : pair * 8 + 8].astype(jnp.bfloat16)
            out_ref[2 * pair, VROWS:, cols] = rows
            out_ref[2 * pair + 1, VROWS:, cols] = rows


def place_kernel(place_ref, back_ref, video_ref, audio_ref):
    core = place_ref[0]
    odd = place_ref[1]
    half_groups = RING // 2
    for j in range(half_groups):
        group = core * half_groups + j
        cols = slice(j * GROUP, (j + 1) * GROUP)
        for s in range(2):
            video_ref[s * VROWS : (s + 1) * VROWS, cols] = back_ref[s, group, :VROWS, :]
        first, second = (back_ref[s, group, VROWS:, :].astype(jnp.float32) for s in range(2))
        low = low_rows(first.shape)
        audio_ref[:, cols] = jnp.where(
            odd == 0,
            jnp.where(low, first, swap_halves(second)),
            jnp.where(low, swap_halves(first), second),
        ).astype(jnp.bfloat16)


def whole(memory_space=pltpu.VMEM):
    return pl.BlockSpec(memory_space=memory_space)


def params():
    return pltpu.CompilerParams(vmem_limit_bytes=VMEM_LIMIT)


def shards(
    video_proj,
    audio_proj,
    video_gains,
    audio_gains,
    cross_gates,
    timestep,
    video_counts,
    audio_counts,
):
    core = lax.axis_index("tp")
    x_count = lax.axis_size("x")
    z_index = lax.axis_index("z")
    parity = lax.axis_index("al")
    packed = pl.pallas_call(
        pack_kernel,
        grid=(1,),
        out_shape=jax.ShapeDtypeStruct((PACK_ROWS, D // 2), jnp.bfloat16),
        in_specs=[
            whole(pltpu.SMEM),
            pl.BlockSpec(video_proj.shape, lambda i: (0, 0, 0)),
            pl.BlockSpec(audio_proj.shape, lambda i: (0, 0, 0)),
            pl.BlockSpec(video_gains.shape, lambda i: (0, 0)),
            pl.BlockSpec(audio_gains.shape, lambda i: (0, 0)),
        ],
        out_specs=pl.BlockSpec((PACK_ROWS, D // 2), lambda i: (0, 0)),
        compiler_params=pltpu.CompilerParams(vmem_limit_bytes=PACK_VMEM),
        name="pack",
    )(core[None], video_proj, audio_proj, video_gains, audio_gains)
    packed = lax.all_gather(packed, "tp", axis=0)
    blocks = pl.pallas_call(
        norm_kernel,
        out_shape=jax.ShapeDtypeStruct((RING, 2 * BLOCK, GROUP), jnp.bfloat16),
        in_specs=[whole(pltpu.SMEM)] + [whole()] * 5,
        out_specs=whole(),
        compiler_params=params(),
        name="norm",
    )(core[None], video_proj, audio_proj, video_gains, audio_gains, packed)

    x_index = lax.axis_index("x")
    halves = jnp.stack([core, 1 - core])

    def allowed(counts):
        here = counts.reshape(YH, x_count, RING)
        return lax.dynamic_index_in_dim(here, x_index, 1, keepdims=False)

    def bias(live):
        return jnp.where(live, 0.0, MASKED).astype(jnp.float32).reshape(1, -1)

    allowed_video, allowed_audio = allowed(video_counts), allowed(audio_counts)
    biases = []
    for al in (parity, 1 - parity):
        aud = np.arange(AH) * AL + al
        video_first = (
            aud[None, :, None] * (2 * VROWS)
            + halves[:, None, None] * VROWS
            + np.arange(VROWS)[None, None, :]
        )
        audio_first = aud[:, None] * 8 + np.arange(8)[None, :]
        biases.append(
            (
                bias(video_first[:, None, :, None, :] < allowed_video[None, :, None, :, None]),
                bias(audio_first[None, :, None, :] < allowed_audio[:, None, :, None]),
            )
        )
    places = jnp.stack([core, z_index % 2])
    gates = lax.dynamic_index_in_dim(cross_gates, timestep[0], 1, keepdims=False)
    gates, packed = lax.optimization_barrier((gates, packed))
    gates = lax.all_gather(gates, "tp", axis=0)
    gates = lax.dynamic_slice(
        gates,
        (z_index // (RING // 2), 0, (z_index % (RING // 2)) * GROUP),
        (1, 2, GROUP),
    )[0].astype(jnp.float32)
    blocks = lax.all_to_all(blocks, "z", split_axis=0, concat_axis=0)
    keyval, queries = blocks[:, :BLOCK], blocks[:, BLOCK:]
    biases = [jnp.concatenate(part, axis=1) for part in zip(*biases)]
    keyval, queries, gates, biases, places = lax.optimization_barrier(
        (keyval, queries, gates, biases, places)
    )
    keyval = lax.all_gather(keyval, ("yh", "ah"), axis=0, tiled=True)
    keyval, queries = lax.optimization_barrier((keyval, queries))
    queries = lax.all_gather(queries, "x", axis=0)
    full_shape = (YH, AH, RING, BLOCK, GROUP)

    y_count = YH * AH * AL
    ways = [
        (y * 2 + c, (y + 1 - 2 * c) % y_count * 2 + c) for y in range(y_count) for c in range(2)
    ]
    swap = [(0, 1), (1, 0)]
    far = lax.ppermute(keyval, ("yh", "ah", "al", "tp"), ways)
    near, queries = lax.optimization_barrier((keyval, queries))
    keyval_other = lax.ppermute(near, "tp", swap)
    far, queries = lax.optimization_barrier((far, queries))
    far_other = lax.ppermute(far, "tp", swap)
    near = [keyval.reshape(full_shape), keyval_other.reshape(full_shape)]
    far = [far.reshape(full_shape), far_other.reshape(full_shape)]

    keyval_spec = pl.BlockSpec(full_shape[:-1] + (HD,), lambda h: (0, 0, 0, 0, h))
    partial = pl.pallas_call(
        attend_kernel,
        grid=(HEADS_HERE,),
        out_shape=jax.ShapeDtypeStruct(
            (x_count, OUT_ROWS + STAT_ROWS, GROUP), jnp.bfloat16
        ),
        in_specs=[
            whole(pltpu.SMEM),
            pl.BlockSpec((x_count, RING, BLOCK, HD), lambda h: (0, 0, 0, h)),
            *[keyval_spec] * 4,
            *[pl.BlockSpec(bias.shape, lambda h: (0, 0)) for bias in biases],
        ],
        out_specs=pl.BlockSpec((x_count, OUT_ROWS + STAT_ROWS, HD), lambda h: (0, 0, h)),
        compiler_params=params(),
        name="attend",
    )(core[None], queries, *near, *far, *biases)
    partial = lax.all_to_all(partial, "x", split_axis=0, concat_axis=0)
    back = pl.pallas_call(
        combine_kernel,
        out_shape=jax.ShapeDtypeStruct((RING, BACK_ROWS, GROUP), jnp.bfloat16),
        in_specs=[whole(), whole()],
        out_specs=whole(),
        compiler_params=params(),
        name="combine",
    )(partial, gates)
    back = lax.all_to_all(back, "z", split_axis=0, concat_axis=0)
    back = lax.all_gather(back, "tp", axis=0)
    return pl.pallas_call(
        place_kernel,
        out_shape=(
            jax.ShapeDtypeStruct((2 * VROWS, D // 2), jnp.bfloat16),
            jax.ShapeDtypeStruct((2 * AROWS, D // 2), jnp.bfloat16),
        ),
        in_specs=[whole(pltpu.SMEM), whole()],
        out_specs=(whole(), whole()),
        compiler_params=params(),
        name="place",
    )(places, back)


def solution(mesh):
    vid = mesh.devices.shape[0]
    cut = (YH, vid // (YH * RING), RING, AH, AL, 2)
    axes = ("yh", "x", "z", "ah", "al", "tp")
    fine = Mesh(mesh.devices.reshape(cut), axes)
    tokens = axes[:-1]
    in_specs = (
        P(None, tokens, "tp"),
        P(None, tokens, "tp"),
        P(None, "tp"),
        P(None, "tp"),
        P(None, None, "tp"),
        P(),
        P(),
        P(),
    )
    out_specs = (P(tokens, "tp"), P(tokens, "tp"))
    return jax.shard_map(
        shards, mesh=fine, in_specs=in_specs, out_specs=out_specs, check_vma=False
    )
```
